512 devices in a mesh: var: 8 (over y_hi, x), tm: 64 (over z, y_lo, core).
Axes of the slice: x: 4, y: 8 (y_hi: 2, y_lo: 4; y = y_hi * 4 + y_lo), z: 8, core: 2. Of those that a mesh axis runs over, the one named last changes fastest.
Arguments:
- frames: bfloat16 [32768, 1024], P('tm'), may hold values from -6 to 6
- span_start: int32 [8], P('var'), parts along dimension 0, may hold values from 0 to 30720
- span_length: int32 [8], P('var'), parts along dimension 0, may hold values from 512 to 2048
- ln_gain: float32 [1024], replicated, may hold values from 0.5 to 2
- w_in: bfloat16 [1024, 2048], P(None, 'tm'), may hold values from -0.1875 to 0.1875
- kernel: float32 [31, 1024], replicated, may hold values from -1 to 1
- bn_scale: float32 [1024], replicated, may hold values from 0.5 to 2
- bn_shift: float32 [1024], replicated, may hold values from -3 to 3
- w_out: bfloat16 [1024, 1024], P(None, 'tm'), may hold values from -0.1875 to 0.1875
Outputs:
- mixed: bfloat16 [262144, 1024], P(('var', 'tm')), parts along dimension 0
The draws below stay inside these ranges and needn't reach their ends.
There are 8 independent parts, one for each index of `var`. The reference program is written for one: setup_inputs(seed, part) draws one part's arguments, and reference() takes and returns one part's arrays. A program takes and returns all parts, laid end to end along the dimension named above; an argument that names none is the same for every part. Nothing has to cross between parts.
Inputs may be any that keep to these rules, and one draw needn't show every extreme that they name: Occluded spans lie inside the sequence: span_start + span_length <= 32768.
All inputs are finite; a program needn't handle non-finite values.
Results may differ from the reference program's by a relative error of at most 0.005.
Values may be sent and summed in bfloat16 or wider, within the bound.
A program may use at most 64 MiB of HBM per device.

```python
import math
import jax
import jax.numpy as jnp
from jax import lax

D = 1024
KERNEL = 31
ROWS_DEV = 512
FRAMES = 32768


def level_of(key, dims, pieces, low, top_value):
    gain, own = 1.0, jax.random.fold_in(key, 6)
    for axis_at, shards_of in pieces:
        heights = jnp.exp(jax.random.uniform(jax.random.fold_in(own, axis_at), (shards_of,), jnp.float32, low / len(pieces), top_value / len(pieces)))
        gain = gain * jnp.repeat(heights, dims[axis_at] // shards_of).reshape([-1 if axis == axis_at else 1 for axis in range(len(dims))])
    return gain


def noise(key, shape, deviation, bound, shards=(), kind=jnp.bfloat16):
    array = jax.random.normal(key, shape, jnp.float32) * deviation
    if len(shards) > 0:
        array = level_of(key, shape, shards, -0.22, 0.18) * array
    return jnp.clip(array, min=-bound, max=bound).astype(kind)


def setup_inputs(seed: int = 0, part: int = 0) -> dict:
    arg_keys = jax.random.split(jax.random.key(seed), 10)
    own_keys = jax.random.split(jax.random.fold_in(arg_keys[9], part), 10)
    return {
        "frames": noise(arg_keys[0], (FRAMES, D), 1.0, 6.0, ((0, 64),)),
        "span_start": jax.random.randint(own_keys[1], (1,), 0, FRAMES - 4 * ROWS_DEV + 1).astype(jnp.int32),
        "span_length": jax.random.randint(own_keys[2], (1,), ROWS_DEV, 4 * ROWS_DEV + 1).astype(jnp.int32),
        "ln_gain": jnp.clip(jnp.exp(jax.random.uniform(arg_keys[3], (D,), jnp.float32, math.log(0.5), math.log(2.0))), 0.5, 2.0),
        "w_in": noise(arg_keys[4], (D, 2 * D), D ** -0.5, 0.1875, ((1, 64),)),
        "kernel": noise(arg_keys[5], (KERNEL, D), KERNEL ** -0.5, 1.0, (), jnp.float32),
        "bn_scale": jnp.clip(jnp.exp(jax.random.uniform(arg_keys[6], (D,), jnp.float32, math.log(0.5), math.log(2.0))), 0.5, 2.0),
        "bn_shift": noise(arg_keys[7], (D,), 0.5, 3.0, (), jnp.float32),
        "w_out": noise(arg_keys[8], (D, D), D ** -0.5, 0.1875, ((1, 64),)),
    }


def normalize(masked, ln_gain):
    values = masked.astype(jnp.float32)
    average = lax.optimization_barrier(jnp.mean(values, axis=1, keepdims=True))
    centred = values - average
    variance = lax.optimization_barrier(jnp.mean(centred * centred, axis=1, keepdims=True))
    return (centred * lax.rsqrt(variance + 1e-05) * ln_gain).astype(jnp.bfloat16)

def reference(frames, span_start, span_length, ln_gain, w_in, kernel, bn_scale, bn_shift, w_out):
    total = frames.shape[0]
    position = jnp.arange(total, dtype=jnp.int32)
    inside = (position >= span_start[0]) & (position < span_start[0] + span_length[0])
    masked = jnp.where(inside[:, None], jnp.zeros((), jnp.bfloat16), frames)
    normed = normalize(masked, ln_gain)
    lifted = jnp.dot(normed, w_in, preferred_element_type=jnp.float32)
    gated = (lifted[:, :D] * jax.nn.sigmoid(lifted[:, D:])).astype(jnp.bfloat16)
    reach = KERNEL // 2
    padded = jnp.pad(gated.astype(jnp.float32), ((reach, reach), (0, 0)))
    convolved = jnp.zeros((total, D), jnp.float32)
    for offset in range(KERNEL):
        convolved = convolved + padded[offset:offset + total] * kernel[offset]
    activated = jax.nn.silu(convolved * bn_scale + bn_shift).astype(jnp.bfloat16)
    branch = jnp.dot(activated, w_out, preferred_element_type=jnp.float32)
    return (masked.astype(jnp.float32) + branch).astype(jnp.bfloat16)
```

```python
import jax
import jax.numpy as jnp
from jax import lax
from jax.experimental import pallas as pl
from jax.experimental.pallas import tpu as pltpu
from jax.sharding import PartitionSpec as P

MESH = pl.DeviceIdType.MESH
BF16, F32 = jnp.bfloat16, jnp.float32
NT = (((1,), (1,)), ((), ()))

ROWS = 512
HALO = 16
SPAN = ROWS + 2 * HALO
D = 1024
TAPS = 31
VAL = 32
OUT = 16
NX, NY, NZ = 4, 4, 8
LN_ROWS = 136
CONV_ROWS = 128


def remote(src, dst, send_sem, recv_sem, device):
    return pltpu.make_async_remote_copy(
        src_ref=src, dst_ref=dst, send_sem=send_sem, recv_sem=recv_sem, device_id=device, device_id_type=MESH
    )


def kernel(
    start_ref, length_ref, frames, w_in, w_out, gain, taps, scale, shift, out,
    fbuf, normed, win, wout, W, WO, G, conv_in, act, acc, obuf,
    local_sem, halo_s, halo_r, zin_s, zin_r, yin_s, yin_r, din_s, din_r,
    x_s, x_r, xf_s, xf_r, zo_s, zo_r, yo_s, yo_r, do_s, do_r,
):
    var, tm = lax.axis_index("var"), lax.axis_index("tm")
    y_hi, x = var // NX, lax.rem(var, NX)
    z, y_lo, core = tm // (2 * NY), lax.rem(tm // 2, NY), lax.rem(tm, 2)
    y = y_hi * NY + y_lo

    def at_y(step):
        there = lax.rem(y + step, 2 * NY)
        return ((there // NY) * NX + x, z * 2 * NY + lax.rem(there, NY) * 2 + core)

    def at_z(step):
        return (var, lax.rem(z + step, NZ) * 2 * NY + y_lo * 2 + core)

    def at_x(step):
        return (y_hi * NX + lax.rem(x + step, NX), tm)

    partner = (var, z * 2 * NY + y_lo * 2 + (1 - core))
    up = jnp.where((core == 1) & (y_lo == NY - 1), 1 - y_hi, y_hi)
    down = jnp.where((core == 0) & (y_lo == 0), 1 - y_hi, y_hi)
    after = (up * NX + x, lax.rem(tm + 1, 2 * NY * NZ))
    before = (down * NX + x, lax.rem(tm + 2 * NY * NZ - 1, 2 * NY * NZ))

    barrier = pltpu.get_barrier_semaphore()
    friends = [at_z(k) for k in range(1, NZ)] + [at_y(1), at_y(2), at_y(6), at_y(7)]
    friends += [at_x(1), at_x(3), partner, after, before]
    for device in friends:
        pl.semaphore_signal(barrier, inc=1, device_id=device, device_id_type=MESH)

    get_in = pltpu.make_async_copy(w_in, win, local_sem.at[0])
    get_out = pltpu.make_async_copy(w_out, wout, local_sem.at[1])
    get_frames = pltpu.make_async_copy(frames, fbuf.at[pl.ds(HALO, ROWS)], local_sem.at[2])
    get_in.start()
    get_out.start()
    get_frames.start()

    role = z // 4
    depth = lax.rem(z - x + NZ, NZ)
    is_source = lax.rem(depth, 4) == 0
    half = y_lo // 2
    slot = lax.rem(y_lo, 2) * 2 + core

    get_in.wait()

    @pl.when(is_source)
    def _():
        W[half, role, slot] = win[...].T

    get_out.wait()
    WO[z, y_lo, core] = wout[...].T
    get_frames.wait()
    pl.semaphore_wait(barrier, len(friends))

    own = W.at[half, role, slot]
    zin = {k: remote(own, own, zin_s.at[k], zin_r.at[role], at_z(k)) for k in range(1, NZ)}

    @pl.when(is_source)
    def _():
        for k in (4, 3, 5, 2, 6, 1, 7):
            zin[k].start()

    tail = remote(fbuf.at[pl.ds(ROWS, HALO)], fbuf.at[pl.ds(0, HALO)], halo_s.at[0], halo_r.at[0], after)
    head = remote(fbuf.at[pl.ds(HALO, HALO)], fbuf.at[pl.ds(HALO + ROWS, HALO)], halo_s.at[1], halo_r.at[1], before)
    tail.start()
    head.start()

    def normalize(row, count, keep):
        values = fbuf[pl.ds(row, count)].astype(F32)
        average = jnp.mean(values, axis=1, keepdims=True)
        centred = values - average
        variance = jnp.mean(centred * centred, axis=1, keepdims=True)
        result = centred * lax.rsqrt(variance + 1e-05) * gain[...]
        if keep is not None:
            result = jnp.where(keep, result, 0.0)
        normed[pl.ds(row, count)] = result.astype(BF16)

    for i in range(ROWS // 128):
        normalize(HALO + i * 128, 128, None)

    near = jnp.where((depth <= 2) | (depth >= 6), 0, 1)

    def yin(r, j):
        s = lax.rem(y_lo + (0, 3, 1, 2)[j], NY)
        piece = W.at[s // 2, r, lax.rem(s, 2) * 2 + core]
        return piece

    def y_copy(r, j):
        device = {1: at_y(1), 2: at_y(7), 3: at_y(2 + 4 * r)}[j]
        return remote(yin(r, 0), yin(r, 0), yin_s.at[r, j], yin_r.at[r, j], device)

    def y_arrival(r, j):
        return remote(yin(r, j), yin(r, j), yin_s.at[r, j], yin_r.at[r, j], partner)

    def core_copy(r, j):
        return remote(yin(r, j), yin(r, j), din_s.at[r, j], din_r.at[r, j], partner)

    def core_arrival(r, j):
        s = lax.rem(y_lo + (0, 3, 1, 2)[j], NY)
        piece = W.at[s // 2, r, lax.rem(s, 2) * 2 + 1 - core]
        return remote(piece, piece, din_s.at[r, j], din_r.at[r, j], partner)

    for r in (near, 1 - near):

        @pl.when(depth != 4 * r)
        def _(r=r):
            piece = yin(r, 0)
            remote(piece, piece, zin_s.at[0], zin_r.at[r], partner).wait_recv()

        for j in (3, 1, 2):
            y_copy(r, j).start()
        core_copy(r, 0).start()

    zo = {k: remote(WO.at[z, y_lo, core], WO.at[z, y_lo, core], zo_s.at[k], zo_r.at[k], at_z(k)) for k in range(1, NZ)}
    for k in (4, 3, 5, 2, 6, 1, 7):
        zo[k].start()

    tail.wait_recv()
    head.wait_recv()
    normalize(0, HALO, tm > 0)
    normalize(HALO + ROWS, HALO, tm < 2 * NY * NZ - 1)

    for j in (1, 2):
        for r in (near, 1 - near):
            y_arrival(r, j).wait_recv()
            core_copy(r, j).start()

    def lift(h):
        columns = jnp.concatenate([W[h, 0].reshape(128, D), W[h, 1].reshape(128, D)], axis=0)
        lifted = lax.dot_general(normed[...], columns, NT, preferred_element_type=F32)
        G[x, h] = (lifted[:, :128] * jax.nn.sigmoid(lifted[:, 128:])).astype(BF16)

    first, second = half, 1 - half

    def x_copy(order, way):
        h = (first, second)[order]
        return remote(G.at[x, h], G.at[x, h], x_s.at[order, way], x_r.at[order, way], at_x((1, 3)[way]))

    def x_arrival(order, way):
        piece = G.at[lax.rem(x + (3, 1)[way], NX), (first, second)[order]]
        return remote(piece, piece, x_s.at[order, way], x_r.at[order, way], partner)

    def x_forward(order):
        piece = G.at[lax.rem(x + (3, 1)[order], NX), (first, second)[order]]
        return remote(piece, piece, xf_s.at[order], xf_r.at[order], at_x((1, 3)[order]))

    def x_far(order):
        piece = G.at[lax.rem(x + 2, NX), (first, second)[order]]
        return remote(piece, piece, xf_s.at[order], xf_r.at[order], partner)

    pair = 2 - lax.rem(y_lo, 2)

    def core_wait(r, j):
        piece = W.at[half, 0, 0]
        remote(piece, piece, din_s.at[r, 0], din_r.at[r, j], partner).wait_recv()

    for r in (0, 1):
        core_arrival(r, 0).wait_recv()
    for r in (0, 1):
        core_wait(r, pair)
    lift(first)
    x_copy(0, 0).start()
    x_copy(0, 1).start()

    for r in (near, 1 - near):
        y_arrival(r, 3).wait_recv()
        core_copy(r, 3).start()
    for r in (0, 1):
        core_wait(r, 3 - pair)
    for r in (0, 1):
        core_arrival(r, 3).wait_recv()
    lift(second)
    x_copy(1, 0).start()
    x_copy(1, 1).start()

    for k in range(1, NZ):
        piece = WO.at[lax.rem(z + NZ - k, NZ), y_lo, core]
        remote(piece, piece, zo_s.at[k], zo_r.at[k], partner).wait_recv()
    line = WO.at[:, y_lo, core]
    low, high = WO.at[pl.ds(0, NZ // 2), y_lo, core], WO.at[pl.ds(NZ // 2, NZ // 2), y_lo, core]
    yo = [
        remote(line, line, yo_s.at[0], yo_r.at[0], at_y(1)),
        remote(line, line, yo_s.at[1], yo_r.at[1], at_y(7)),
        remote(low, low, yo_s.at[2], yo_r.at[2], at_y(2)),
        remote(high, high, yo_s.at[3], yo_r.at[3], at_y(6)),
    ]
    for copy in yo:
        copy.start()

    def out_line(j, c):
        return WO.at[:, lax.rem(y_lo + (0, 3, 1, 2)[j], NY), c]

    def do(j):
        return remote(out_line(j, core), out_line(j, core), do_s.at[j], do_r.at[j], partner)

    do(0).start()

    row0 = tm * ROWS
    span_low, span_high = start_ref[0], start_ref[0] + length_ref[0]

    def occluded(begin, count):
        position = begin + lax.broadcasted_iota(jnp.int32, (count, 1), 0)
        return (position >= span_low) & (position < span_high)

    def convolve(step, order):
        owner, h = lax.rem(x + step, NX), (first, second)[order]
        lanes = pl.ds(pl.multiple_of(owner * 256 + h * 128, 128), 128)
        conv_in[...] = jnp.where(occluded(row0 - HALO, SPAN), 0.0, G[owner, h].astype(F32))

        @pl.loop(0, ROWS // CONV_ROWS)
        def _(i):
            row = pl.multiple_of(i * CONV_ROWS, CONV_ROWS)
            total = None
            for j in range(TAPS):
                term = conv_in[pl.ds(row + j + 1, CONV_ROWS)] * taps[pl.ds(j, 1), lanes]
                total = term if total is None else total + term
            value = total * scale[:, lanes] + shift[:, lanes]
            act[owner, pl.ds(row, CONV_ROWS), pl.ds(pl.multiple_of(h * 128, 128), 128)] = (
                value * jax.nn.sigmoid(value)
            ).astype(BF16)

    def product(step, n):
        owner = lax.rem(x + step, NX)
        depths = pl.ds(pl.multiple_of(owner * 256, 256), 256)
        columns = WO[2 * n : 2 * n + 2, :, :, :, depths].reshape(256, 256)
        return lax.dot_general(act[owner], columns, NT, preferred_element_type=F32)

    convolve(0, 0)
    convolve(0, 1)

    x_arrival(0, 0).wait_recv()
    x_forward(0).start()
    convolve(3, 0)
    x_arrival(0, 1).wait_recv()
    convolve(1, 0)

    for j in (1, 2):
        remote(out_line(j, core), out_line(j, core), yo_s.at[0], yo_r.at[j - 1], partner).wait_recv()
        do(j).start()

    x_arrival(1, 1).wait_recv()
    x_forward(1).start()
    convolve(1, 1)
    x_arrival(1, 0).wait_recv()
    convolve(3, 1)

    far = lax.rem(y_lo + 2, NY)
    for part in (0, 1):
        piece = WO.at[pl.ds(part * 4, 4), far, core]
        remote(piece, piece, yo_s.at[0], yo_r.at[2 + part], partner).wait_recv()
    do(3).start()
    for j in range(4):
        remote(out_line(j, 1 - core), out_line(j, 1 - core), do_s.at[j], do_r.at[j], partner).wait_recv()

    for n in range(4):
        acc[n] = product(0, n)
    for step in (1, 3):
        for n in range(4):
            acc[n] += product(step, n)

    for order in (0, 1):
        x_far(order).wait_recv()
        convolve(2, order)

    results = []
    for n in range(4):
        lanes = pl.ds(n * 256, 256)
        masked = jnp.where(occluded(row0, ROWS), 0.0, fbuf[pl.ds(HALO, ROWS), lanes].astype(F32))
        obuf[:, lanes] = (masked + (acc[n] + product(2, n))).astype(BF16)
        copy = pltpu.make_async_copy(obuf.at[:, lanes], out.at[:, lanes], local_sem.at[3 + n])
        copy.start()
        results.append(copy)

    @pl.when(is_source)
    def _():
        for k in range(1, NZ):
            zin[k].wait_send()

    tail.wait_send()
    head.wait_send()
    for r in (0, 1):
        for j in (1, 2, 3):
            y_copy(r, j).wait_send()
        for j in range(4):
            core_copy(r, j).wait_send()
    for order in (0, 1):
        for way in (0, 1):
            x_copy(order, way).wait_send()
        x_forward(order).wait_send()
    for k in range(1, NZ):
        zo[k].wait_send()
    for copy in yo:
        copy.wait_send()
    for j in range(4):
        do(j).wait_send()
    for copy in results:
        copy.wait()


def module(frames, span_start, span_length, ln_gain, w_in, taps, bn_scale, bn_shift, w_out):
    vmem, smem, hbm = (pl.BlockSpec(memory_space=space) for space in (pltpu.VMEM, pltpu.SMEM, pl.ANY))
    dma = pltpu.SemaphoreType.DMA
    return pl.pallas_call(
        kernel,
        name="conformer_conv",
        out_shape=jax.ShapeDtypeStruct((ROWS, D), BF16),
        in_specs=[smem, smem, hbm, hbm, hbm, vmem, vmem, vmem, vmem],
        out_specs=hbm,
        scratch_shapes=[
            pltpu.VMEM((SPAN, D), BF16),
            pltpu.VMEM((SPAN, D), BF16),
            pltpu.VMEM((D, VAL), BF16),
            pltpu.VMEM((D, OUT), BF16),
            pltpu.VMEM((2, 2, 4, VAL, D), BF16),
            pltpu.VMEM((NZ, NY, 2, OUT, D), BF16),
            pltpu.VMEM((NX, 2, SPAN, 128), BF16),
            pltpu.VMEM((SPAN, 128), F32),
            pltpu.VMEM((NX, ROWS, 256), BF16),
            pltpu.VMEM((4, ROWS, 256), F32),
            pltpu.VMEM((ROWS, D), BF16),
            dma((7,)),
            dma((2,)), dma((2,)),
            dma((NZ,)), dma((2,)),
            dma((2, 4)), dma((2, 4)),
            dma((2, 4)), dma((2, 4)),
            dma((2, 2)), dma((2, 2)),
            dma((2,)), dma((2,)),
            dma((NZ,)), dma((NZ,)),
            dma((4,)), dma((4,)),
            dma((4,)), dma((4,)),
        ],
        compiler_params=pltpu.CompilerParams(
            collective_id=0, has_side_effects=True, vmem_limit_bytes=40 * 1024 * 1024
        ),
    )(
        span_start, span_length, frames, w_in, w_out, ln_gain.reshape(1, D), taps,
        bn_scale.reshape(1, D), bn_shift.reshape(1, D),
    )


def solution(mesh):
    return jax.shard_map(
        module,
        mesh=mesh,
        in_specs=(P("tm", None), P("var"), P("var"), P(), P(None, "tm"), P(), P(), P(), P(None, "tm")),
        out_specs=P(("var", "tm"), None),
        check_vma=False,
    )
```

```python
import jax
import jax.numpy as jnp
from jax import lax
from jax.experimental import pallas as pl
from jax.experimental.pallas import tpu as pltpu
from jax.sharding import PartitionSpec as P

MESH = pl.DeviceIdType.MESH
BF16, F32 = jnp.bfloat16, jnp.float32
NT = (((1,), (1,)), ((), ()))

ROWS = 512
HALO = 16
SPAN = ROWS + 2 * HALO
D = 1024
TAPS = 31
VAL = 32
OUT = 16
NX, NY, NZ = 4, 4, 8
LB = 384
VMEM_BYTES = 58 * 1024 * 1024
CONV_ROWS = 128


def remote(src, dst, send_sem, recv_sem, device):
    return pltpu.make_async_remote_copy(
        src_ref=src, dst_ref=dst, send_sem=send_sem, recv_sem=recv_sem, device_id=device, device_id_type=MESH
    )


def kernel(
    start_hbm, length_hbm, frames, w_in, w_out, gain_hbm, taps_hbm, scale_hbm, shift_hbm, out,
    fbuf, normed, win, wout, W, WO, G, conv_in, act, acc, obuf, gain, raw_taps, raw_scale, raw_shift, params, start, length,
    local_sem, halo_s, halo_r, zin_s, zin_r, yin_s, yin_r, din_s, din_r,
    x_s, x_r, xf_s, xf_r, zo_s, zo_r, xo_s, xo_r, yo_s, yo_r, do_s, do_r,
    yb_s, yb_r, zb_s, zb_r, db_s, db_r,
):
    var, tm = lax.axis_index("var"), lax.axis_index("tm")
    y_hi, x = var // NX, lax.rem(var, NX)
    z, y_lo, core = tm // (2 * NY), lax.rem(tm // 2, NY), lax.rem(tm, 2)
    y = y_hi * NY + y_lo

    def at_y(step):
        there = lax.rem(y + step, 2 * NY)
        return ((there // NY) * NX + x, z * 2 * NY + lax.rem(there, NY) * 2 + core)

    def at_z(step):
        return (var, lax.rem(z + step, NZ) * 2 * NY + y_lo * 2 + core)

    def at_x(step):
        return (y_hi * NX + lax.rem(x + step, NX), tm)

    partner = (var, z * 2 * NY + y_lo * 2 + (1 - core))
    up = jnp.where((core == 1) & (y_lo == NY - 1), 1 - y_hi, y_hi)
    down = jnp.where((core == 0) & (y_lo == 0), 1 - y_hi, y_hi)
    after = (up * NX + x, lax.rem(tm + 1, 2 * NY * NZ))
    before = (down * NX + x, lax.rem(tm + 2 * NY * NZ - 1, 2 * NY * NZ))

    barrier = pltpu.get_barrier_semaphore()
    friends = [at_z(k) for k in (4, 3, 5, 2, 6, 1, 7)] + [at_y(2), at_y(6), at_y(1), at_y(7)]
    friends += [at_x(2), at_x(1), at_x(3), after, before, partner]
    for device in friends:
        pl.semaphore_signal(barrier, inc=1, device_id=device, device_id_type=MESH)

    fetch = [
        pltpu.make_async_copy(src, dst, local_sem.at[i])
        for i, (src, dst) in enumerate(
            (
                (w_in, win),
                (w_out, wout),
                (frames, fbuf.at[pl.ds(HALO, ROWS)]),
                (taps_hbm, raw_taps),
                (scale_hbm, raw_scale),
                (shift_hbm, raw_shift),
                (gain_hbm, gain),
                (start_hbm, start),
                (length_hbm, length),
            )
        )
    ]
    for copy in fetch:
        copy.start()

    role = z // 4
    depth = lax.rem(z - x + NZ, NZ)
    is_source = lax.rem(depth, 4) == 0

    old = lax.broadcasted_iota(jnp.int32, (256, 256), 0)
    new = lax.broadcasted_iota(jnp.int32, (256, 256), 1)
    order = (old // 32 == (new // 16) % 8) & ((old // 16) % 2 == new // 128) & (old % 16 == new % 16)
    order = jnp.where(order, 1.0, 0.0)

    fetch[0].wait()

    @pl.when(is_source)
    def _():
        W[0, role, y_lo, core] = win[:16]
        W[1, role, y_lo, core] = win[16:]

    fetch[1].wait()
    for b in range(4):
        lanes = pl.ds(b * 256, 256)
        wout[:, lanes] = jnp.dot(wout[:, lanes], order.astype(BF16), preferred_element_type=F32).astype(BF16)
    WO[z, y_lo, core, :, :LB] = wout[:, :LB]

    @pl.when(is_source)
    def _():
        WO[z, y_lo, core, :, LB:] = wout[:, LB:]

    fetch[2].wait()
    pl.semaphore_wait(barrier, len(friends))

    back = pl.ds(LB, D - LB)
    front = pl.ds(0, LB)
    far_first = (4, 3, 5, 2, 6, 1, 7)

    def zin(c, k):
        piece = W.at[c, role, y_lo, core]
        return remote(piece, piece, zin_s.at[c, k], zin_r.at[c, role], at_z(k))

    def zo(k):
        piece = WO.at[z, y_lo, core, :, back]
        return remote(piece, piece, zo_s.at[k], zo_r.at[role], at_z(k))

    @pl.when(is_source)
    def _():
        for c in (0, 1):
            for k in far_first:
                zin(c, k).start()
        for k in far_first:
            zo(k).start()

    def yb(j):
        piece = WO.at[z, y_lo, core, :, front]
        return remote(piece, piece, yb_s.at[j], yb_r.at[j], at_y((0, 1, 7, 2)[j]))

    for j in (3, 1, 2):
        yb(j).start()

    tail = remote(fbuf.at[pl.ds(ROWS, HALO)], fbuf.at[pl.ds(0, HALO)], halo_s.at[0], halo_r.at[0], after)
    head = remote(fbuf.at[pl.ds(HALO, HALO)], fbuf.at[pl.ds(HALO + ROWS, HALO)], halo_s.at[1], halo_r.at[1], before)
    tail.start()
    head.start()

    for copy in fetch[3:]:
        copy.wait()
    for b in range(4):
        lanes = pl.ds(b * 256, 256)
        for first, src in ((0, raw_taps), (32, raw_scale), (40, raw_shift)):
            params[pl.ds(first, src.shape[0]), lanes] = jnp.dot(
                src[:, lanes], order, precision=lax.Precision.HIGHEST, preferred_element_type=F32
            )

    def normalize(row, count, keep):
        values = fbuf[pl.ds(row, count)].astype(F32)
        average = jnp.mean(values, axis=1, keepdims=True)
        centred = values - average
        variance = jnp.mean(centred * centred, axis=1, keepdims=True)
        result = centred * lax.rsqrt(variance + 1e-05) * gain[...]
        if keep is not None:
            result = jnp.where(keep, result, 0.0)
        normed[pl.ds(row, count)] = result.astype(BF16)

    for i in range(ROWS // 128):
        normalize(HALO + i * 128, 128, None)
    tail.wait_recv()
    head.wait_recv()
    normalize(0, HALO, tm > 0)
    normalize(HALO + ROWS, HALO, tm < 2 * NY * NZ - 1)

    near = jnp.where((depth <= 2) | (depth >= 6), 0, 1)
    roles = (near, 1 - near)

    def line(j):
        return lax.rem(y_lo + (0, 3, 1, 2)[j], NY)

    def yin(c, r, j):
        piece = W.at[c, r, y_lo, core]
        device = {1: at_y(1), 2: at_y(7), 3: at_y(2 + 4 * r)}[j]
        return remote(piece, piece, yin_s.at[c, r, j], yin_r.at[c, r, j], device)

    def yin_arrival(c, r, j):
        piece = W.at[c, r, line(j), core]
        return remote(piece, piece, yin_s.at[c, r, j], yin_r.at[c, r, j], partner)

    def din(c, r, j):
        piece = W.at[c, r, line(j), core]
        return remote(piece, piece, din_s.at[c, r, j], din_r.at[c, r, j], partner)

    def din_arrival(c, r, j):
        piece = W.at[c, r, line(j), 1 - core]
        return remote(piece, piece, din_s.at[c, r, j], din_r.at[c, r, j], partner)

    for c in (0, 1):
        for r in roles:

            @pl.when(depth != 4 * r)
            def _(c=c, r=r):
                piece = W.at[c, r, y_lo, core]
                remote(piece, piece, zin_s.at[c, 0], zin_r.at[c, r], partner).wait_recv()

            for j in (3, 1, 2):
                yin(c, r, j).start()
            din(c, r, 0).start()

    def xo(r, w):
        piece = WO.at[x + 4 * r, y_lo, core, :, back]
        return remote(piece, piece, xo_s.at[r, w], xo_r.at[r, w], at_x((2, 1, 3)[w]))

    for r in (0, 1):

        @pl.when(depth != 4 * r)
        def _(r=r):
            piece = WO.at[x + 4 * r, y_lo, core, :, back]
            remote(piece, piece, zo_s.at[0], zo_r.at[r], partner).wait_recv()

        for w in range(3):
            xo(r, w).start()

    for j in (1, 2, 3):
        piece = WO.at[z, line(j), core, :, front]
        remote(piece, piece, yb_s.at[j], yb_r.at[j], partner).wait_recv()

    def zb(k):
        piece = WO.at[z, :, core, :, front]
        return remote(piece, piece, zb_s.at[k], zb_r.at[k], at_z(k))

    for k in far_first:
        zb(k).start()

    def lift(c):
        columns = jnp.concatenate([W[c, 0].reshape(128, D), W[c, 1].reshape(128, D)], axis=0)
        lifted = lax.dot_general(normed[...], columns, NT, preferred_element_type=F32)
        G[x, c] = (lifted[:, :128] * jax.nn.sigmoid(lifted[:, 128:])).astype(BF16)

    parts = (pl.ds(0, SPAN // 2), pl.ds(SPAN // 2, SPAN // 2))

    def x_copy(c, way, p):
        piece = G.at[x, c, parts[p]]
        return remote(piece, piece, x_s.at[c, way, p], x_r.at[c, way, p], at_x((1, 3)[way]))

    def x_arrival(c, way, p):
        piece = G.at[lax.rem(x + (3, 1)[way], NX), c, parts[p]]
        return remote(piece, piece, x_s.at[c, way, p], x_r.at[c, way, p], partner)

    def x_forward(c, p):
        piece = G.at[lax.rem(x + (3, 1)[p], NX), c, parts[p]]
        return remote(piece, piece, xf_s.at[c, p], xf_r.at[c, p], at_x((1, 3)[p]))

    def x_far(c, p):
        piece = G.at[lax.rem(x + 2, NX), c, parts[p]]
        return remote(piece, piece, xf_s.at[c, p], xf_r.at[c, p], partner)

    def lift_and_send(c):
        for j in (1, 2, 3):
            for r in roles:
                yin_arrival(c, r, j).wait_recv()
                din(c, r, j).start()
        for j in range(4):
            for r in (0, 1):
                din_arrival(c, r, j).wait_recv()
        lift(c)
        for p in (0, 1):
            for way in (0, 1):
                x_copy(c, way, p ^ way).start()

    lift_and_send(0)

    for w in range(3):
        for r in (0, 1):
            piece = WO.at[lax.rem(x + (2, 3, 1)[w], NX) + 4 * r, y_lo, core, :, back]
            remote(piece, piece, xo_s.at[r, w], xo_r.at[r, w], partner).wait_recv()

    full = WO.at[:, y_lo, core, :, back]
    low, high = WO.at[pl.ds(0, NZ // 2), y_lo, core, :, back], WO.at[pl.ds(NZ // 2, NZ // 2), y_lo, core, :, back]
    yo = [
        remote(low, low, yo_s.at[2], yo_r.at[2], at_y(2)),
        remote(high, high, yo_s.at[3], yo_r.at[3], at_y(6)),
        remote(full, full, yo_s.at[0], yo_r.at[0], at_y(1)),
        remote(full, full, yo_s.at[1], yo_r.at[1], at_y(7)),
    ]
    for copy in yo:
        copy.start()

    def do(j):
        piece = WO.at[:, line(j), core, :, back]
        return remote(piece, piece, do_s.at[j], do_r.at[j], partner)

    do(0).start()

    lift_and_send(1)

    row0 = tm * ROWS
    span_low, span_high = start[0], start[0] + length[0]

    def occluded(begin, count):
        position = begin + lax.broadcasted_iota(jnp.int32, (count, 1), 0)
        return (position >= span_low) & (position < span_high)

    def convolve(step, c):
        owner = lax.rem(x + step, NX)
        lanes = pl.ds(pl.multiple_of(owner * 256 + c * 128, 128), 128)
        conv_in[...] = jnp.where(occluded(row0 - HALO, SPAN), 0.0, G[owner, c].astype(F32))

        @pl.loop(0, ROWS // CONV_ROWS)
        def _(i):
            row = pl.multiple_of(i * CONV_ROWS, CONV_ROWS)
            total = None
            for j in range(TAPS):
                term = conv_in[pl.ds(row + j + 1, CONV_ROWS)] * params[pl.ds(j, 1), lanes]
                total = term if total is None else total + term
            value = total * params[pl.ds(32, 1), lanes] + params[pl.ds(40, 1), lanes]
            act[owner, pl.ds(row, CONV_ROWS), pl.ds(c * 128, 128)] = (value * jax.nn.sigmoid(value)).astype(BF16)

    def product(step, n):
        owner = lax.rem(x + step, NX)
        depths = pl.ds(pl.multiple_of(owner * 256, 256), 256)
        columns = WO[2 * n : 2 * n + 2, :, :, :, depths].reshape(256, 256)
        return lax.dot_general(act[owner], columns, NT, preferred_element_type=F32)

    convolve(0, 0)
    convolve(0, 1)
    for p in (0, 1):
        x_arrival(0, p, p).wait_recv()
        x_forward(0, p).start()
    for p in (0, 1):
        x_arrival(0, p, 1 - p).wait_recv()
    convolve(1, 0)
    convolve(3, 0)

    for p in (0, 1):
        x_arrival(1, p, p).wait_recv()
        x_forward(1, p).start()

    for k in range(1, NZ):
        piece = WO.at[lax.rem(z + NZ - k, NZ), :, core, :, front]
        remote(piece, piece, zb_s.at[k], zb_r.at[k], partner).wait_recv()
    mine = WO.at[:, :, core, :, front]
    db = remote(mine, mine, db_s.at[0], db_r.at[0], partner)
    db.start()

    for p in (0, 1):
        x_arrival(1, p, 1 - p).wait_recv()
    convolve(1, 1)
    convolve(3, 1)

    for j in (1, 2):
        piece = WO.at[:, line(j), core, :, back]
        remote(piece, piece, yo_s.at[0], yo_r.at[j - 1], partner).wait_recv()
        do(j).start()
    for h in (0, 1):
        piece = WO.at[pl.ds(h * 4, 4), line(3), core, :, back]
        remote(piece, piece, yo_s.at[0], yo_r.at[2 + h], partner).wait_recv()
    do(3).start()

    for p in (0, 1):
        x_far(0, p).wait_recv()
    convolve(2, 0)

    for j in range(4):
        piece = WO.at[:, line(j), 1 - core, :, back]
        remote(piece, piece, do_s.at[j], do_r.at[j], partner).wait_recv()
    theirs = WO.at[:, :, 1 - core, :, front]
    remote(theirs, theirs, db_s.at[0], db_r.at[0], partner).wait_recv()

    for n in range(4):
        acc[n] = product(0, n)
    for step in (1, 3):
        for n in range(4):
            acc[n] += product(step, n)

    for p in (0, 1):
        x_far(1, p).wait_recv()
    convolve(2, 1)

    results = []
    for n in range(4):
        lanes = pl.ds(n * 256, 256)
        masked = jnp.where(occluded(row0, ROWS), 0.0, fbuf[pl.ds(HALO, ROWS), lanes].astype(F32))
        obuf[:, lanes] = (masked + (acc[n] + product(2, n))).astype(BF16)
        copy = pltpu.make_async_copy(obuf.at[:, lanes], out.at[:, lanes], local_sem.at[9 + n])
        copy.start()
        results.append(copy)

    @pl.when(is_source)
    def _():
        for k in far_first:
            zin(0, k).wait_send()
            zin(1, k).wait_send()
            zo(k).wait_send()

    tail.wait_send()
    head.wait_send()
    for c in (0, 1):
        for r in (0, 1):
            for j in (1, 2, 3):
                yin(c, r, j).wait_send()
            for j in range(4):
                din(c, r, j).wait_send()
        for p in (0, 1):
            for way in (0, 1):
                x_copy(c, way, p).wait_send()
            x_forward(c, p).wait_send()
    for r in (0, 1):
        for w in range(3):
            xo(r, w).wait_send()
    for j in (1, 2, 3):
        yb(j).wait_send()
    for k in far_first:
        zb(k).wait_send()
    for copy in yo:
        copy.wait_send()
    for j in range(4):
        do(j).wait_send()
    db.wait_send()
    for copy in results:
        copy.wait()


def module(frames, span_start, span_length, ln_gain, w_in, taps, bn_scale, bn_shift, w_out):
    hbm = pl.BlockSpec(memory_space=pl.ANY)
    dma = pltpu.SemaphoreType.DMA
    return pl.pallas_call(
        kernel,
        name="conformer_conv",
        out_shape=jax.ShapeDtypeStruct((ROWS, D), BF16),
        in_specs=[hbm] * 9,
        out_specs=hbm,
        scratch_shapes=[
            pltpu.VMEM((SPAN, D), BF16),
            pltpu.VMEM((SPAN, D), BF16),
            pltpu.VMEM((VAL, D), BF16),
            pltpu.VMEM((OUT, D), BF16),
            pltpu.VMEM((2, 2, NY, 2, OUT, D), BF16),
            pltpu.VMEM((NZ, NY, 2, OUT, D), BF16),
            pltpu.VMEM((NX, 2, SPAN, 128), BF16),
            pltpu.VMEM((SPAN, 128), F32),
            pltpu.VMEM((NX, ROWS, 256), BF16),
            pltpu.VMEM((4, ROWS, 256), F32),
            pltpu.VMEM((ROWS, D), BF16),
            pltpu.VMEM((1, D), F32),
            pltpu.VMEM((TAPS, D), F32),
            pltpu.VMEM((1, D), F32),
            pltpu.VMEM((1, D), F32),
            pltpu.VMEM((48, D), F32),
            pltpu.SMEM((1,), jnp.int32),
            pltpu.SMEM((1,), jnp.int32),
            dma((13,)),
            dma((2,)), dma((2,)),
            dma((2, NZ)), dma((2, 2)),
            dma((2, 2, 4)), dma((2, 2, 4)),
            dma((2, 2, 4)), dma((2, 2, 4)),
            dma((2, 2, 2)), dma((2, 2, 2)),
            dma((2, 2)), dma((2, 2)),
            dma((NZ,)), dma((2,)),
            dma((2, 3)), dma((2, 3)),
            dma((4,)), dma((4,)),
            dma((4,)), dma((4,)),
            dma((4,)), dma((4,)),
            dma((NZ,)), dma((NZ,)),
            dma((1,)), dma((1,)),
        ],
        compiler_params=pltpu.CompilerParams(
            collective_id=0, has_side_effects=True, vmem_limit_bytes=VMEM_BYTES
        ),
    )(
        span_start, span_length, frames, w_in.T, w_out.T, ln_gain.reshape(1, D), taps,
        bn_scale.reshape(1, D), bn_shift.reshape(1, D),
    )


def solution(mesh):
    return jax.shard_map(
        module,
        mesh=mesh,
        in_specs=(P("tm", None), P("var"), P("var"), P(), P(None, "tm"), P(), P(), P(), P(None, "tm")),
        out_specs=P(("var", "tm"), None),
        check_vma=False,
    )
```

```python
import jax
import jax.numpy as jnp
from jax import lax
from jax.experimental import pallas as pl
from jax.experimental.pallas import tpu as pltpu
from jax.sharding import PartitionSpec as P

MESH = pl.DeviceIdType.MESH
BF16, F32 = jnp.bfloat16, jnp.float32
NT = (((1,), (1,)), ((), ()))

ROWS = 512
HALO = 16
SPAN = ROWS + 2 * HALO
D = 1024
TAPS = 31
VAL = 32
OUT = 16
NX, NY, NZ = 4, 4, 8
LB = 384
VMEM_BYTES = 58 * 1024 * 1024
CONV_ROWS = 128


def remote(src, dst, send_sem, recv_sem, device):
    return pltpu.make_async_remote_copy(
        src_ref=src, dst_ref=dst, send_sem=send_sem, recv_sem=recv_sem, device_id=device, device_id_type=MESH
    )


def kernel(
    start_hbm, length_hbm, frames, w_in, w_out, gain_hbm, taps_hbm, scale_hbm, shift_hbm, out,
    fbuf, normed, win, wout, W, WO, G, conv_in, act, acc, gain, raw_taps, raw_scale, raw_shift, params, start, length,
    local_sem, halo_s, halo_r, zin_s, zin_r, yin_s, yin_r, din_s, din_r,
    x_s, x_r, xf_s, xf_r, zo_s, zo_r, xo_s, xo_r, yo_s, yo_r, do_s, do_r,
    yb_s, yb_r, zb_s, zb_r, db_s, db_r,
):
    var, tm = lax.axis_index("var"), lax.axis_index("tm")
    y_hi, x = var // NX, lax.rem(var, NX)
    z, y_lo, core = tm // (2 * NY), lax.rem(tm // 2, NY), lax.rem(tm, 2)
    y = y_hi * NY + y_lo

    def at_y(step):
        there = lax.rem(y + step, 2 * NY)
        return ((there // NY) * NX + x, z * 2 * NY + lax.rem(there, NY) * 2 + core)

    def at_z(step):
        return (var, lax.rem(z + step, NZ) * 2 * NY + y_lo * 2 + core)

    def at_x(step):
        return (y_hi * NX + lax.rem(x + step, NX), tm)

    partner = (var, z * 2 * NY + y_lo * 2 + (1 - core))
    up = jnp.where((core == 1) & (y_lo == NY - 1), 1 - y_hi, y_hi)
    down = jnp.where((core == 0) & (y_lo == 0), 1 - y_hi, y_hi)
    after = (up * NX + x, lax.rem(tm + 1, 2 * NY * NZ))
    before = (down * NX + x, lax.rem(tm + 2 * NY * NZ - 1, 2 * NY * NZ))

    barrier = pltpu.get_barrier_semaphore()
    friends = [at_z(k) for k in (4, 3, 5, 2, 6, 1, 7)] + [at_y(2), at_y(6), at_y(1), at_y(7)]
    friends += [at_x(2), at_x(1), at_x(3), after, before, partner]
    for device in friends:
        pl.semaphore_signal(barrier, inc=1, device_id=device, device_id_type=MESH)

    fetch = [
        pltpu.make_async_copy(src, dst, local_sem.at[i])
        for i, (src, dst) in enumerate(
            (
                (w_in, win),
                (w_out, wout),
                (frames, fbuf.at[pl.ds(HALO, ROWS)]),
                (taps_hbm, raw_taps),
                (scale_hbm, raw_scale),
                (shift_hbm, raw_shift),
                (gain_hbm, gain),
                (start_hbm, start),
                (length_hbm, length),
            )
        )
    ]
    for copy in fetch:
        copy.start()

    role = z // 4
    depth = lax.rem(z - x + NZ, NZ)
    is_source = lax.rem(depth, 4) == 0

    old = lax.broadcasted_iota(jnp.int32, (256, 256), 0)
    new = lax.broadcasted_iota(jnp.int32, (256, 256), 1)
    order = (old // 32 == (new // 16) % 8) & ((old // 16) % 2 == new // 128) & (old % 16 == new % 16)
    order = jnp.where(order, 1.0, 0.0)

    fetch[0].wait()

    @pl.when(is_source)
    def _():
        W[0, role, y_lo, core] = win[:16]
        W[1, role, y_lo, core] = win[16:]

    fetch[1].wait()
    for b in range(4):
        lanes = pl.ds(b * 256, 256)
        wout[:, lanes] = jnp.dot(wout[:, lanes], order.astype(BF16), preferred_element_type=F32).astype(BF16)
    WO[z, y_lo, core, :, :LB] = wout[:, :LB]

    @pl.when(is_source)
    def _():
        WO[z, y_lo, core, :, LB:] = wout[:, LB:]

    fetch[2].wait()
    pl.semaphore_wait(barrier, len(friends))

    back = pl.ds(LB, D - LB)
    front = pl.ds(0, LB)
    far_first = (4, 3, 5, 2, 6, 1, 7)

    def zin(c, k):
        piece = W.at[c, role, y_lo, core]
        return remote(piece, piece, zin_s.at[c, k], zin_r.at[c, role], at_z(k))

    def zo(k):
        piece = WO.at[z, y_lo, core, :, back]
        return remote(piece, piece, zo_s.at[k], zo_r.at[role], at_z(k))

    @pl.when(is_source)
    def _():
        for c in (0, 1):
            for k in far_first:
                zin(c, k).start()
        for k in far_first:
            zo(k).start()

    def yb(j):
        piece = WO.at[z, y_lo, core, :, front]
        return remote(piece, piece, yb_s.at[j], yb_r.at[j], at_y((0, 1, 7, 2)[j]))

    for j in (3, 1, 2):
        yb(j).start()

    tail = remote(fbuf.at[pl.ds(ROWS, HALO)], fbuf.at[pl.ds(0, HALO)], halo_s.at[0], halo_r.at[0], after)
    head = remote(fbuf.at[pl.ds(HALO, HALO)], fbuf.at[pl.ds(HALO + ROWS, HALO)], halo_s.at[1], halo_r.at[1], before)
    tail.start()
    head.start()

    for copy in fetch[3:]:
        copy.wait()
    for b in range(4):
        lanes = pl.ds(b * 256, 256)
        for first, src in ((0, raw_taps), (32, raw_scale), (40, raw_shift)):
            params[pl.ds(first, src.shape[0]), lanes] = jnp.dot(
                src[:, lanes], order, precision=lax.Precision.HIGHEST, preferred_element_type=F32
            )

    def normalize(row, count, keep):
        values = fbuf[pl.ds(row, count)].astype(F32)
        average = jnp.mean(values, axis=1, keepdims=True)
        centred = values - average
        variance = jnp.mean(centred * centred, axis=1, keepdims=True)
        result = centred * lax.rsqrt(variance + 1e-05) * gain[...]
        if keep is not None:
            result = jnp.where(keep, result, 0.0)
        normed[pl.ds(row, count)] = result.astype(BF16)

    for i in range(ROWS // 128):
        normalize(HALO + i * 128, 128, None)
    tail.wait_recv()
    head.wait_recv()
    normalize(0, HALO, tm > 0)
    normalize(HALO + ROWS, HALO, tm < 2 * NY * NZ - 1)

    near = jnp.where((depth <= 2) | (depth >= 6), 0, 1)
    roles = (near, 1 - near)

    def line(j):
        return lax.rem(y_lo + (0, 3, 1, 2)[j], NY)

    def yin(c, r, j):
        piece = W.at[c, r, y_lo, core]
        device = {1: at_y(1), 2: at_y(7), 3: at_y(2 + 4 * r)}[j]
        return remote(piece, piece, yin_s.at[c, r, j], yin_r.at[c, r, j], device)

    def yin_arrival(c, r, j):
        piece = W.at[c, r, line(j), core]
        return remote(piece, piece, yin_s.at[c, r, j], yin_r.at[c, r, j], partner)

    def din(c, r, j):
        piece = W.at[c, r, line(j), core]
        return remote(piece, piece, din_s.at[c, r, j], din_r.at[c, r, j], partner)

    def din_arrival(c, r, j):
        piece = W.at[c, r, line(j), 1 - core]
        return remote(piece, piece, din_s.at[c, r, j], din_r.at[c, r, j], partner)

    for c in (0, 1):
        for r in roles:

            @pl.when(depth != 4 * r)
            def _(c=c, r=r):
                piece = W.at[c, r, y_lo, core]
                remote(piece, piece, zin_s.at[c, 0], zin_r.at[c, r], partner).wait_recv()

            for j in (3, 1, 2):
                yin(c, r, j).start()
            din(c, r, 0).start()

    def xo(r, w):
        piece = WO.at[x + 4 * r, y_lo, core, :, back]
        return remote(piece, piece, xo_s.at[r, w], xo_r.at[r, w], at_x((2, 1, 3)[w]))

    for r in (0, 1):

        @pl.when(depth != 4 * r)
        def _(r=r):
            piece = WO.at[x + 4 * r, y_lo, core, :, back]
            remote(piece, piece, zo_s.at[0], zo_r.at[r], partner).wait_recv()

        for w in range(3):
            xo(r, w).start()

    for j in (1, 2, 3):
        piece = WO.at[z, line(j), core, :, front]
        remote(piece, piece, yb_s.at[j], yb_r.at[j], partner).wait_recv()

    def zb(k):
        piece = WO.at[z, :, core, :, front]
        return remote(piece, piece, zb_s.at[k], zb_r.at[k], at_z(k))

    for k in far_first:
        zb(k).start()

    def lift(c):
        columns = jnp.concatenate([W[c, 0].reshape(128, D), W[c, 1].reshape(128, D)], axis=0)
        lifted = lax.dot_general(normed[...], columns, NT, preferred_element_type=F32)
        G[x, c] = (lifted[:, :128] * jax.nn.sigmoid(lifted[:, 128:])).astype(BF16)

    parts = (pl.ds(0, SPAN // 2), pl.ds(SPAN // 2, SPAN // 2))

    def x_copy(c, way, p):
        piece = G.at[x, c, parts[p]]
        return remote(piece, piece, x_s.at[c, way, p], x_r.at[c, way, p], at_x((1, 3)[way]))

    def x_arrival(c, way, p):
        piece = G.at[lax.rem(x + (3, 1)[way], NX), c, parts[p]]
        return remote(piece, piece, x_s.at[c, way, p], x_r.at[c, way, p], partner)

    def x_forward(c, p):
        piece = G.at[lax.rem(x + (3, 1)[p], NX), c, parts[p]]
        return remote(piece, piece, xf_s.at[c, p], xf_r.at[c, p], at_x((1, 3)[p]))

    def x_far(c, p):
        piece = G.at[lax.rem(x + 2, NX), c, parts[p]]
        return remote(piece, piece, xf_s.at[c, p], xf_r.at[c, p], partner)

    def lift_and_send(c):
        for j in (1, 2, 3):
            for r in roles:
                yin_arrival(c, r, j).wait_recv()
                din(c, r, j).start()
        for j in range(4):
            for r in (0, 1):
                din_arrival(c, r, j).wait_recv()
        lift(c)
        for p in (0, 1):
            for way in (0, 1):
                x_copy(c, way, p ^ way).start()

    lift_and_send(0)

    for w in range(3):
        for r in (0, 1):
            piece = WO.at[lax.rem(x + (2, 3, 1)[w], NX) + 4 * r, y_lo, core, :, back]
            remote(piece, piece, xo_s.at[r, w], xo_r.at[r, w], partner).wait_recv()

    full = WO.at[:, y_lo, core, :, back]
    low, high = WO.at[pl.ds(0, NZ // 2), y_lo, core, :, back], WO.at[pl.ds(NZ // 2, NZ // 2), y_lo, core, :, back]
    yo = [
        remote(low, low, yo_s.at[2], yo_r.at[2], at_y(2)),
        remote(high, high, yo_s.at[3], yo_r.at[3], at_y(6)),
        remote(full, full, yo_s.at[0], yo_r.at[0], at_y(1)),
        remote(full, full, yo_s.at[1], yo_r.at[1], at_y(7)),
    ]
    for copy in yo:
        copy.start()

    def do(j):
        piece = WO.at[:, line(j), core, :, back]
        return remote(piece, piece, do_s.at[j], do_r.at[j], partner)

    do(0).start()

    lift_and_send(1)

    row0 = tm * ROWS
    span_low, span_high = start[0], start[0] + length[0]

    def occluded(begin, count):
        position = begin + lax.broadcasted_iota(jnp.int32, (count, 1), 0)
        return (position >= span_low) & (position < span_high)

    def convolve(step, c):
        owner = lax.rem(x + step, NX)
        lanes = pl.ds(pl.multiple_of(owner * 256 + c * 128, 128), 128)
        conv_in[...] = jnp.where(occluded(row0 - HALO, SPAN), 0.0, G[owner, c].astype(F32))

        @pl.loop(0, ROWS // CONV_ROWS)
        def _(i):
            row = pl.multiple_of(i * CONV_ROWS, CONV_ROWS)
            total = None
            for j in range(TAPS):
                term = conv_in[pl.ds(row + j + 1, CONV_ROWS)] * params[pl.ds(j, 1), lanes]
                total = term if total is None else total + term
            value = total * params[pl.ds(32, 1), lanes] + params[pl.ds(40, 1), lanes]
            act[owner, pl.ds(row, CONV_ROWS), pl.ds(c * 128, 128)] = (value * jax.nn.sigmoid(value)).astype(BF16)

    def product(step, n):
        owner = lax.rem(x + step, NX)
        depths = pl.ds(pl.multiple_of(owner * 256, 256), 256)
        columns = WO[2 * n : 2 * n + 2, :, :, :, depths].reshape(256, 256)
        return lax.dot_general(act[owner], columns, NT, preferred_element_type=F32)

    convolve(0, 0)
    convolve(0, 1)
    for p in (0, 1):
        x_arrival(0, p, p).wait_recv()
        x_forward(0, p).start()
    for p in (0, 1):
        x_arrival(0, p, 1 - p).wait_recv()
    convolve(1, 0)
    convolve(3, 0)

    for p in (0, 1):
        x_arrival(1, p, p).wait_recv()
        x_forward(1, p).start()

    for k in range(1, NZ):
        piece = WO.at[lax.rem(z + NZ - k, NZ), :, core, :, front]
        remote(piece, piece, zb_s.at[k], zb_r.at[k], partner).wait_recv()
    mine = WO.at[:, :, core, :, front]
    db = remote(mine, mine, db_s.at[0], db_r.at[0], partner)
    db.start()

    for p in (0, 1):
        x_arrival(1, p, 1 - p).wait_recv()
    convolve(1, 1)
    convolve(3, 1)

    for j in (1, 2):
        piece = WO.at[:, line(j), core, :, back]
        remote(piece, piece, yo_s.at[0], yo_r.at[j - 1], partner).wait_recv()
        do(j).start()
    for h in (0, 1):
        piece = WO.at[pl.ds(h * 4, 4), line(3), core, :, back]
        remote(piece, piece, yo_s.at[0], yo_r.at[2 + h], partner).wait_recv()
    do(3).start()

    for p in (0, 1):
        x_far(0, p).wait_recv()
    convolve(2, 0)

    for j in range(4):
        piece = WO.at[:, line(j), 1 - core, :, back]
        remote(piece, piece, do_s.at[j], do_r.at[j], partner).wait_recv()
    theirs = WO.at[:, :, 1 - core, :, front]
    remote(theirs, theirs, db_s.at[0], db_r.at[0], partner).wait_recv()

    for n in range(4):
        acc[n] = product(0, n)
    for step in (1, 3):
        for n in range(4):
            acc[n] += product(step, n)

    for p in (0, 1):
        x_far(1, p).wait_recv()
    convolve(2, 1)

    for n in range(4):
        lanes = pl.ds(n * 256, 256)
        masked = jnp.where(occluded(row0, ROWS), 0.0, fbuf[pl.ds(HALO, ROWS), lanes].astype(F32))
        out[:, lanes] = (masked + (acc[n] + product(2, n))).astype(BF16)

    @pl.when(is_source)
    def _():
        for k in far_first:
            zin(0, k).wait_send()
            zin(1, k).wait_send()
            zo(k).wait_send()

    tail.wait_send()
    head.wait_send()
    for c in (0, 1):
        for r in (0, 1):
            for j in (1, 2, 3):
                yin(c, r, j).wait_send()
            for j in range(4):
                din(c, r, j).wait_send()
        for p in (0, 1):
            for way in (0, 1):
                x_copy(c, way, p).wait_send()
            x_forward(c, p).wait_send()
    for r in (0, 1):
        for w in range(3):
            xo(r, w).wait_send()
    for j in (1, 2, 3):
        yb(j).wait_send()
    for k in far_first:
        zb(k).wait_send()
    for copy in yo:
        copy.wait_send()
    for j in range(4):
        do(j).wait_send()
    db.wait_send()


def module(frames, span_start, span_length, ln_gain, w_in, taps, bn_scale, bn_shift, w_out):
    hbm = pl.BlockSpec(memory_space=pl.ANY)
    dma = pltpu.SemaphoreType.DMA
    return pl.pallas_call(
        kernel,
        name="conformer_conv",
        out_shape=pltpu.VMEM((ROWS, D), BF16),
        in_specs=[hbm] * 9,
        out_specs=pl.BlockSpec(memory_space=pltpu.VMEM),
        scratch_shapes=[
            pltpu.VMEM((SPAN, D), BF16),
            pltpu.VMEM((SPAN, D), BF16),
            pltpu.VMEM((VAL, D), BF16),
            pltpu.VMEM((OUT, D), BF16),
            pltpu.VMEM((2, 2, NY, 2, OUT, D), BF16),
            pltpu.VMEM((NZ, NY, 2, OUT, D), BF16),
            pltpu.VMEM((NX, 2, SPAN, 128), BF16),
            pltpu.VMEM((SPAN, 128), F32),
            pltpu.VMEM((NX, ROWS, 256), BF16),
            pltpu.VMEM((4, ROWS, 256), F32),
            pltpu.VMEM((1, D), F32),
            pltpu.VMEM((TAPS, D), F32),
            pltpu.VMEM((1, D), F32),
            pltpu.VMEM((1, D), F32),
            pltpu.VMEM((48, D), F32),
            pltpu.SMEM((1,), jnp.int32),
            pltpu.SMEM((1,), jnp.int32),
            dma((9,)),
            dma((2,)), dma((2,)),
            dma((2, NZ)), dma((2, 2)),
            dma((2, 2, 4)), dma((2, 2, 4)),
            dma((2, 2, 4)), dma((2, 2, 4)),
            dma((2, 2, 2)), dma((2, 2, 2)),
            dma((2, 2)), dma((2, 2)),
            dma((NZ,)), dma((2,)),
            dma((2, 3)), dma((2, 3)),
            dma((4,)), dma((4,)),
            dma((4,)), dma((4,)),
            dma((4,)), dma((4,)),
            dma((NZ,)), dma((NZ,)),
            dma((1,)), dma((1,)),
        ],
        compiler_params=pltpu.CompilerParams(
            collective_id=0, has_side_effects=True, vmem_limit_bytes=VMEM_BYTES
        ),
    )(
        span_start, span_length, frames, w_in.T, w_out.T, ln_gain.reshape(1, D), taps,
        bn_scale.reshape(1, D), bn_shift.reshape(1, D),
    )


def solution(mesh):
    return jax.shard_map(
        module,
        mesh=mesh,
        in_specs=(P("tm", None), P("var"), P("var"), P(), P(None, "tm"), P(), P(), P(), P(None, "tm")),
        out_specs=P(("var", "tm"), None),
        check_vma=False,
    )
```

```python
import jax
import jax.numpy as jnp
from jax import lax
from jax.experimental import pallas as pl
from jax.experimental.pallas import tpu as pltpu
from jax.sharding import PartitionSpec as P

MESH = pl.DeviceIdType.MESH
BF16, F32 = jnp.bfloat16, jnp.float32
NT = (((1,), (1,)), ((), ()))

ROWS = 512
HALO = 16
SPAN = ROWS + 2 * HALO
D = 1024
TAPS = 31
OUT = 16
NX, NY, NZ = 4, 4, 8
LB = 512
VMEM_BYTES = 58 * 1024 * 1024
CONV_ROWS = 256


def remote(src, dst, send_sem, recv_sem, device):
    return pltpu.make_async_remote_copy(
        src_ref=src, dst_ref=dst, send_sem=send_sem, recv_sem=recv_sem, device_id=device, device_id_type=MESH
    )


def kernel(
    start_hbm, length_hbm, frames, w_in, w_out, gain_hbm, taps_hbm, scale_hbm, shift_hbm, out,
    fbuf, normed, wout, W, WO, G, conv_in, act, acc, gain, raw_taps, raw_scale, raw_shift, params, start, length,
    local_sem, halo_s, halo_r, zin_s, zin_r, yin_s, yin_r, din_s, din_r,
    x_s, x_r, xf_s, xf_r, zo_s, zo_r, xo_s, xo_r, yo_s, yo_r, do_s, do_r,
    yb_s, yb_r, zb_s, zb_r, db_s, db_r,
):
    var, tm = lax.axis_index("var"), lax.axis_index("tm")
    y_hi, x = var // NX, lax.rem(var, NX)
    z, y_lo, core = tm // (2 * NY), lax.rem(tm // 2, NY), lax.rem(tm, 2)
    y = y_hi * NY + y_lo

    def at_y(step):
        there = lax.rem(y + step, 2 * NY)
        return ((there // NY) * NX + x, z * 2 * NY + lax.rem(there, NY) * 2 + core)

    def at_z(step):
        return (var, lax.rem(z + step, NZ) * 2 * NY + y_lo * 2 + core)

    def at_x(step):
        return (y_hi * NX + lax.rem(x + step, NX), tm)

    partner = (var, z * 2 * NY + y_lo * 2 + (1 - core))
    up = jnp.where((core == 1) & (y_lo == NY - 1), 1 - y_hi, y_hi)
    down = jnp.where((core == 0) & (y_lo == 0), 1 - y_hi, y_hi)
    after = (up * NX + x, lax.rem(tm + 1, 2 * NY * NZ))
    before = (down * NX + x, lax.rem(tm + 2 * NY * NZ - 1, 2 * NY * NZ))

    barrier = pltpu.get_barrier_semaphore()
    friends = [at_z(k) for k in (2, 6, 1, 7)] + [at_y(2), at_y(6), at_y(1), at_y(7)]
    friends += [at_x(2), at_x(1), at_x(3), after, before, partner]
    for device in friends:
        pl.semaphore_signal(barrier, inc=1, device_id=device, device_id_type=MESH)

    fetch = [
        pltpu.make_async_copy(src, dst, local_sem.at[i])
        for i, (src, dst) in enumerate(
            (
                (w_out, wout),
                (frames, fbuf.at[pl.ds(HALO, ROWS)]),
                (taps_hbm, raw_taps),
                (scale_hbm, raw_scale),
                (shift_hbm, raw_shift),
                (gain_hbm, gain),
                (start_hbm, start),
                (length_hbm, length),
            )
        )
    ]
    for copy in fetch:
        copy.start()

    role = z // 4
    depth = lax.rem(z - x + NZ, NZ)
    is_source = lax.rem(depth, 4) == 0

    pieces = ((0, pl.ds(0, D // 2)), (0, pl.ds(D // 2, D // 2)), (1, pl.ds(0, D)))
    two_steps = (2, 6, 1, 7)

    def own_slot(i):
        c, lanes = pieces[i]
        return pltpu.make_async_copy(
            w_in.at[pl.ds(c * OUT, OUT), lanes], W.at[c, role, y_lo, core, :, lanes], local_sem.at[9 + i]
        )

    def zin(i, k):
        c, lanes = pieces[i]
        return remote(
            w_in.at[pl.ds(c * OUT, OUT), lanes], W.at[c, role, y_lo, core, :, lanes],
            zin_s.at[i, k], zin_r.at[i, role], at_z(k),
        )

    @pl.when(is_source)
    def _():
        for i in range(3):
            own_slot(i).start()

    pl.semaphore_wait(barrier, len(friends))

    @pl.when(is_source)
    def _():
        for i in (0, 1):
            for k in two_steps:
                zin(i, k).start()

    old = lax.broadcasted_iota(jnp.int32, (256, 256), 0)
    new = lax.broadcasted_iota(jnp.int32, (256, 256), 1)
    order = (old // 32 == (new // 16) % 8) & ((old // 16) % 2 == new // 128) & (old % 16 == new % 16)
    order = jnp.where(order, 1.0, 0.0)

    back = pl.ds(LB, D - LB)
    front = pl.ds(0, LB)

    fetch[0].wait()
    for b in range(4):
        lanes = pl.ds(b * 256, 256)
        wout[:, lanes] = jnp.dot(wout[:, lanes], order.astype(BF16), preferred_element_type=F32).astype(BF16)
    WO[z, y_lo, core, :, :LB] = wout[:, :LB]

    def zo(k):
        piece = WO.at[z, y_lo, core, :, back]
        return remote(piece, piece, zo_s.at[k], zo_r.at[role], at_z(k))

    @pl.when(is_source)
    def _():
        WO[z, y_lo, core, :, LB:] = wout[:, LB:]
        for k in two_steps:
            zo(k).start()
        for k in two_steps:
            zin(2, k).start()

    def yb(j):
        piece = WO.at[z, y_lo, core, :, front]
        return remote(piece, piece, yb_s.at[j], yb_r.at[j], at_y((0, 1, 7, 2)[j]))

    for j in (3, 1, 2):
        yb(j).start()

    fetch[1].wait()
    tail = remote(fbuf.at[pl.ds(ROWS, HALO)], fbuf.at[pl.ds(0, HALO)], halo_s.at[0], halo_r.at[0], after)
    head = remote(fbuf.at[pl.ds(HALO, HALO)], fbuf.at[pl.ds(HALO + ROWS, HALO)], halo_s.at[1], halo_r.at[1], before)
    tail.start()
    head.start()

    for copy in fetch[2:]:
        copy.wait()
    for b in range(4):
        lanes = pl.ds(b * 256, 256)
        for first, src in ((0, raw_taps), (32, raw_scale), (40, raw_shift)):
            params[pl.ds(first, src.shape[0]), lanes] = jnp.dot(
                src[:, lanes], order, precision=lax.Precision.HIGHEST, preferred_element_type=F32
            )

    def normalize(row, count, keep):
        values = fbuf[pl.ds(row, count)].astype(F32)
        average = jnp.mean(values, axis=1, keepdims=True)
        centred = values - average
        variance = jnp.mean(centred * centred, axis=1, keepdims=True)
        result = centred * lax.rsqrt(variance + 1e-05) * gain[...]
        if keep is not None:
            result = jnp.where(keep, result, 0.0)
        normed[pl.ds(row, count)] = result.astype(BF16)

    for i in (0, 1):
        normalize(HALO + i * 128, 128, None)

    near = jnp.where((depth <= 2) | (depth >= 6), 0, 1)
    roles = (near, 1 - near)

    def line(j):
        return lax.rem(y_lo + (0, 3, 1, 2)[j], NY)

    def yin(i, r, j):
        c, lanes = pieces[i]
        piece = W.at[c, r, y_lo, core, :, lanes]
        device = {1: at_y(1), 2: at_y(7), 3: at_y(2 + 4 * r)}[j]
        return remote(piece, piece, yin_s.at[i, r, j], yin_r.at[i, r, j], device)

    def yin_arrival(i, r, j):
        c, lanes = pieces[i]
        piece = W.at[c, r, line(j), core, :, lanes]
        return remote(piece, piece, yin_s.at[i, r, j], yin_r.at[i, r, j], partner)

    def din(c, r, j):
        piece = W.at[c, r, line(j), core]
        return remote(piece, piece, din_s.at[c, r, j], din_r.at[c, r, j], partner)

    def din_arrival(c, r, j):
        piece = W.at[c, r, line(j), 1 - core]
        return remote(piece, piece, din_s.at[c, r, j], din_r.at[c, r, j], partner)

    def relay(r, piece, send_sem, recv_sem):
        @pl.when(depth == 2 + 4 * r)
        def _():
            remote(piece, piece, send_sem(3), recv_sem, at_z(1)).start()
            remote(piece, piece, send_sem(4), recv_sem, at_z(2)).start()

        @pl.when(depth == 6 - 4 * r)
        def _():
            remote(piece, piece, send_sem(5), recv_sem, at_z(7)).start()

    def pass_on(i):
        c, lanes = pieces[i]
        for r in roles:
            piece = W.at[c, r, y_lo, core, :, lanes]

            @pl.when(depth == 4 * r)
            def _():
                own_slot(i).wait()

            @pl.when(depth != 4 * r)
            def _(r=r, piece=piece):
                remote(piece, piece, zin_s.at[i, 0], zin_r.at[i, r], partner).wait_recv()

            relay(r, piece, lambda k: zin_s.at[i, k], zin_r.at[i, r])
            for j in (3, 1, 2):
                yin(i, r, j).start()
            if i:
                din(i - 1, r, 0).start()

    def xo(r, w):
        piece = WO.at[x + 4 * r, y_lo, core, :, back]
        return remote(piece, piece, xo_s.at[r, w], xo_r.at[r, w], at_x((2, 1, 3)[w]))

    def pass_back():
        for r in roles:
            piece = WO.at[x + 4 * r, y_lo, core, :, back]

            @pl.when(depth != 4 * r)
            def _(r=r, piece=piece):
                remote(piece, piece, zo_s.at[0], zo_r.at[r], partner).wait_recv()

            relay(r, piece, lambda k: zo_s.at[k], zo_r.at[r])
            for w in range(3):
                xo(r, w).start()

    pass_on(0)
    pass_on(1)
    pass_back()
    normalize(HALO + 256, 128, None)
    pass_on(2)

    for j in (1, 2, 3):
        piece = WO.at[z, line(j), core, :, front]
        remote(piece, piece, yb_s.at[j], yb_r.at[j], partner).wait_recv()

    def zb_piece(k, base):
        rows = {4: pl.ds(0, 2), 0: pl.ds(2, 2)}.get(k, pl.ds(0, NY))
        return WO.at[lax.rem(base + NZ - (k or 4), NZ), rows, core, :, front]

    def zb(k):
        step = {3: 1, 5: 7, 4: 2, 0: 6}.get(k, k)
        piece = zb_piece(k, lax.rem(z + step, NZ))
        return remote(piece, piece, zb_s.at[k], zb_r.at[k], at_z(step))

    def zb_arrival(k):
        piece = zb_piece(k, z)
        return remote(piece, piece, zb_s.at[k], zb_r.at[k], partner)

    for k in (1, 7, 2, 6):
        zb(k).start()

    normalize(HALO + 384, 128, None)
    tail.wait_recv()
    head.wait_recv()
    normalize(0, HALO, tm > 0)
    normalize(HALO + ROWS, HALO, tm < 2 * NY * NZ - 1)

    def lift(c):
        columns = jnp.concatenate([W[c, 0].reshape(128, D), W[c, 1].reshape(128, D)], axis=0)
        lifted = lax.dot_general(normed[...], columns, NT, preferred_element_type=F32)
        G[x, c] = (lifted[:, :128] * jax.nn.sigmoid(lifted[:, 128:])).astype(BF16)

    parts = (pl.ds(0, SPAN // 2), pl.ds(SPAN // 2, SPAN // 2))

    def x_copy(c, way, p):
        piece = G.at[x, c, parts[p]]
        return remote(piece, piece, x_s.at[c, way, p], x_r.at[c, way, p], at_x((1, 3)[way]))

    def x_arrival(c, way, p):
        piece = G.at[lax.rem(x + (3, 1)[way], NX), c, parts[p]]
        return remote(piece, piece, x_s.at[c, way, p], x_r.at[c, way, p], partner)

    def x_forward(c, p):
        piece = G.at[lax.rem(x + (3, 1)[p], NX), c, parts[p]]
        return remote(piece, piece, xf_s.at[c, p], xf_r.at[c, p], at_x((1, 3)[p]))

    def x_far(c, p):
        piece = G.at[lax.rem(x + 2, NX), c, parts[p]]
        return remote(piece, piece, xf_s.at[c, p], xf_r.at[c, p], partner)

    row0 = tm * ROWS
    span_low, span_high = start[0], start[0] + length[0]

    def occluded(begin, count):
        position = begin + lax.broadcasted_iota(jnp.int32, (count, 1), 0)
        return (position >= span_low) & (position < span_high)

    def convolve(step, c):
        owner = lax.rem(x + step, NX)
        lanes = pl.ds(pl.multiple_of(owner * 256 + c * 128, 128), 128)
        conv_in[...] = jnp.where(occluded(row0 - HALO, SPAN), 0.0, G[owner, c].astype(F32))

        @pl.loop(0, ROWS // CONV_ROWS)
        def _(i):
            row = pl.multiple_of(i * CONV_ROWS, CONV_ROWS)
            total = None
            for j in range(TAPS):
                term = conv_in[pl.ds(row + j + 1, CONV_ROWS)] * params[pl.ds(j, 1), lanes]
                total = term if total is None else total + term
            value = total * params[pl.ds(32, 1), lanes] + params[pl.ds(40, 1), lanes]
            act[owner, pl.ds(row, CONV_ROWS), pl.ds(c * 128, 128)] = (value * jax.nn.sigmoid(value)).astype(BF16)

    def product(step, n, first=0, count=256):
        owner = lax.rem(x + step, NX)
        depths = pl.ds(pl.multiple_of(owner * 256 + first, 128), count)
        columns = WO[2 * n : 2 * n + 2, :, :, :, depths].reshape(256, count)
        return lax.dot_general(act[owner, :, first : first + count], columns, NT, preferred_element_type=F32)

    def gather_core(c):
        for j in (1, 2, 3):
            for r in roles:
                for i in (0, 1) if c == 0 else (2,):
                    yin_arrival(i, r, j).wait_recv()
                din(c, r, j).start()

    def lift_and_send(c):
        for j in range(4):
            for r in (0, 1):
                din_arrival(c, r, j).wait_recv()
        lift(c)
        for p in (0, 1):
            for way in (0, 1):
                x_copy(c, way, p ^ way).start()

    gather_core(0)
    lift_and_send(0)

    for w in range(3):
        for r in (0, 1):
            piece = WO.at[lax.rem(x + (2, 3, 1)[w], NX) + 4 * r, y_lo, core, :, back]
            remote(piece, piece, xo_s.at[r, w], xo_r.at[r, w], partner).wait_recv()

    full = WO.at[:, y_lo, core, :, back]
    low, high = WO.at[pl.ds(0, NZ // 2), y_lo, core, :, back], WO.at[pl.ds(NZ // 2, NZ // 2), y_lo, core, :, back]
    yo = [
        remote(low, low, yo_s.at[2], yo_r.at[2], at_y(2)),
        remote(high, high, yo_s.at[3], yo_r.at[3], at_y(6)),
        remote(full, full, yo_s.at[0], yo_r.at[0], at_y(1)),
        remote(full, full, yo_s.at[1], yo_r.at[1], at_y(7)),
    ]
    for copy in yo:
        copy.start()

    def do(j):
        piece = WO.at[:, line(j), core, :, back]
        return remote(piece, piece, do_s.at[j], do_r.at[j], partner)

    do(0).start()

    gather_core(1)
    lift_and_send(1)

    for k in (1, 7, 2, 6):
        zb_arrival(k).wait_recv()
    for k in (4, 0, 3, 5):
        zb(k).start()

    for p in (0, 1):
        x_arrival(0, p, p).wait_recv()
        x_forward(0, p).start()
    convolve(0, 0)
    convolve(0, 1)
    for p in (0, 1):
        x_arrival(0, p, 1 - p).wait_recv()
    convolve(1, 0)
    convolve(3, 0)
    for p in (0, 1):
        x_arrival(1, p, p).wait_recv()
        x_forward(1, p).start()

    for j in (1, 2):
        piece = WO.at[:, line(j), core, :, back]
        remote(piece, piece, yo_s.at[0], yo_r.at[j - 1], partner).wait_recv()
        do(j).start()
    for p in (0, 1):
        x_arrival(1, p, 1 - p).wait_recv()
    convolve(1, 1)
    for h in (0, 1):
        piece = WO.at[pl.ds(h * 4, 4), line(3), core, :, back]
        remote(piece, piece, yo_s.at[0], yo_r.at[2 + h], partner).wait_recv()
    do(3).start()
    for k in (3, 5, 4, 0):
        zb_arrival(k).wait_recv()
    mine = WO.at[:, :, core, :, front]
    db = remote(mine, mine, db_s.at[0], db_r.at[0], partner)
    db.start()
    convolve(3, 1)

    for p in (0, 1):
        x_far(0, p).wait_recv()
    convolve(2, 0)

    for j in range(4):
        piece = WO.at[:, line(j), 1 - core, :, back]
        remote(piece, piece, do_s.at[j], do_r.at[j], partner).wait_recv()
    theirs = WO.at[:, :, 1 - core, :, front]
    remote(theirs, theirs, db_s.at[0], db_r.at[0], partner).wait_recv()

    for n in range(4):
        acc[n] = product(0, n) + product(1, n) + product(3, n) + product(2, n, 0, 128)

    for p in (0, 1):
        x_far(1, p).wait_recv()
    convolve(2, 1)

    for n in range(4):
        lanes = pl.ds(n * 256, 256)
        masked = jnp.where(occluded(row0, ROWS), 0.0, fbuf[pl.ds(HALO, ROWS), lanes].astype(F32))
        out[:, lanes] = (masked + (acc[n] + product(2, n, 128, 128))).astype(BF16)

    @pl.when(is_source)
    def _():
        for k in two_steps:
            for i in range(3):
                zin(i, k).wait_send()
            zo(k).wait_send()

    @pl.when(lax.rem(depth, 4) == 2)
    def _():
        back_piece = WO.at[z, y_lo, core, :, back]
        for k in (3, 4, 5):
            for i, (c, lanes) in enumerate(pieces):
                piece = W.at[c, role, y_lo, core, :, lanes]
                remote(piece, piece, zin_s.at[i, k], zin_r.at[i, 0], partner).wait_send()
            remote(back_piece, back_piece, zo_s.at[k], zo_r.at[0], partner).wait_send()

    tail.wait_send()
    head.wait_send()
    for c in (0, 1):
        for r in (0, 1):
            for j in range(4):
                din(c, r, j).wait_send()
        for p in (0, 1):
            for way in (0, 1):
                x_copy(c, way, p).wait_send()
            x_forward(c, p).wait_send()
    for r in (0, 1):
        for j in (1, 2, 3):
            for i in range(3):
                yin(i, r, j).wait_send()
        for w in range(3):
            xo(r, w).wait_send()
    for j in (1, 2, 3):
        yb(j).wait_send()
    for k in range(NZ):
        zb(k).wait_send()
    for copy in yo:
        copy.wait_send()
    for j in range(4):
        do(j).wait_send()
    db.wait_send()


def module(frames, span_start, span_length, ln_gain, w_in, taps, bn_scale, bn_shift, w_out):
    hbm = pl.BlockSpec(memory_space=pl.ANY)
    dma = pltpu.SemaphoreType.DMA
    return pl.pallas_call(
        kernel,
        name="conformer_conv",
        out_shape=pltpu.VMEM((ROWS, D), BF16),
        in_specs=[hbm] * 9,
        out_specs=pl.BlockSpec(memory_space=pltpu.VMEM),
        scratch_shapes=[
            pltpu.VMEM((SPAN, D), BF16),
            pltpu.VMEM((SPAN, D), BF16),
            pltpu.VMEM((OUT, D), BF16),
            pltpu.VMEM((2, 2, NY, 2, OUT, D), BF16),
            pltpu.VMEM((NZ, NY, 2, OUT, D), BF16),
            pltpu.VMEM((NX, 2, SPAN, 128), BF16),
            pltpu.VMEM((SPAN, 128), F32),
            pltpu.VMEM((NX, ROWS, 256), BF16),
            pltpu.VMEM((4, ROWS, 256), F32),
            pltpu.VMEM((1, D), F32),
            pltpu.VMEM((TAPS, D), F32),
            pltpu.VMEM((1, D), F32),
            pltpu.VMEM((1, D), F32),
            pltpu.VMEM((48, D), F32),
            pltpu.SMEM((1,), jnp.int32),
            pltpu.SMEM((1,), jnp.int32),
            dma((12,)),
            dma((2,)), dma((2,)),
            dma((3, NZ)), dma((3, 2)),
            dma((3, 2, 4)), dma((3, 2, 4)),
            dma((2, 2, 4)), dma((2, 2, 4)),
            dma((2, 2, 2)), dma((2, 2, 2)),
            dma((2, 2)), dma((2, 2)),
            dma((NZ,)), dma((2,)),
            dma((2, 3)), dma((2, 3)),
            dma((4,)), dma((4,)),
            dma((4,)), dma((4,)),
            dma((4,)), dma((4,)),
            dma((NZ,)), dma((NZ,)),
            dma((1,)), dma((1,)),
        ],
        compiler_params=pltpu.CompilerParams(
            collective_id=0, has_side_effects=True, vmem_limit_bytes=VMEM_BYTES
        ),
    )(
        span_start, span_length, frames, w_in.T, w_out.T, ln_gain.reshape(1, D), taps,
        bn_scale.reshape(1, D), bn_shift.reshape(1, D),
    )


def solution(mesh):
    return jax.shard_map(
        module,
        mesh=mesh,
        in_specs=(P("tm", None), P("var"), P("var"), P(), P(None, "tm"), P(), P(), P(), P(None, "tm")),
        out_specs=P(("var", "tm"), None),
        check_vma=False,
    )
```

```python
import jax
import jax.numpy as jnp
from jax import lax
from jax.experimental import pallas as pl
from jax.experimental.pallas import tpu as pltpu
from jax.sharding import PartitionSpec as P

MESH = pl.DeviceIdType.MESH
BF16, F32 = jnp.bfloat16, jnp.float32
NT = (((1,), (1,)), ((), ()))

ROWS = 512
HALO = 16
SPAN = ROWS + 2 * HALO
D = 1024
TAPS = 31
VAL = 32
OUT = 16
NX, NY, NZ = 4, 4, 8
LB = 512
VMEM_BYTES = 58 * 1024 * 1024
CONV_ROWS = 256


def sigmoid(values):
    return 0.5 + 0.5 * jnp.tanh(0.5 * values)


def remote(src, dst, send_sem, recv_sem, device):
    return pltpu.make_async_remote_copy(
        src_ref=src, dst_ref=dst, send_sem=send_sem, recv_sem=recv_sem, device_id=device, device_id_type=MESH
    )


def kernel(
    start_hbm, length_hbm, frames, w_in, w_out, gain_hbm, taps_hbm, scale_hbm, shift_hbm, out,
    fbuf, normed, win, wout, W, WO, G, conv_in, act, acc, gain, raw_taps, raw_scale, raw_shift, params, start, length,
    local_sem, halo_s, halo_r, zin_s, zin_r, yin_s, yin_r, din_s, din_r,
    x_s, x_r, xf_s, xf_r, zo_s, zo_r, xo_s, xo_r, yo_s, yo_r, do_s, do_r,
    yb_s, yb_r, zb_s, zb_r, db_s, db_r,
):
    var, tm = lax.axis_index("var"), lax.axis_index("tm")
    y_hi, x = var // NX, lax.rem(var, NX)
    z, y_lo, core = tm // (2 * NY), lax.rem(tm // 2, NY), lax.rem(tm, 2)
    y = y_hi * NY + y_lo

    def at_y(step):
        there = lax.rem(y + step, 2 * NY)
        return ((there // NY) * NX + x, z * 2 * NY + lax.rem(there, NY) * 2 + core)

    def at_z(step):
        return (var, lax.rem(z + step, NZ) * 2 * NY + y_lo * 2 + core)

    def at_x(step):
        return (y_hi * NX + lax.rem(x + step, NX), tm)

    partner = (var, z * 2 * NY + y_lo * 2 + (1 - core))
    up = jnp.where((core == 1) & (y_lo == NY - 1), 1 - y_hi, y_hi)
    down = jnp.where((core == 0) & (y_lo == 0), 1 - y_hi, y_hi)
    after = (up * NX + x, lax.rem(tm + 1, 2 * NY * NZ))
    before = (down * NX + x, lax.rem(tm + 2 * NY * NZ - 1, 2 * NY * NZ))

    barrier = pltpu.get_barrier_semaphore()
    friends = [at_z(k) for k in (4, 3, 5, 2, 6, 1, 7)] + [at_y(2), at_y(6), at_y(1), at_y(7)]
    friends += [at_x(2), at_x(1), at_x(3), after, before, partner]
    for device in friends:
        pl.semaphore_signal(barrier, inc=1, device_id=device, device_id_type=MESH)

    fetch = [
        pltpu.make_async_copy(src, dst, local_sem.at[i])
        for i, (src, dst) in enumerate(
            (
                (w_in, win),
                (w_out, wout),
                (frames, fbuf.at[pl.ds(HALO, ROWS)]),
                (taps_hbm, raw_taps),
                (scale_hbm, raw_scale),
                (shift_hbm, raw_shift),
                (gain_hbm, gain),
                (start_hbm, start),
                (length_hbm, length),
            )
        )
    ]
    for copy in fetch:
        copy.start()

    role = z // 4
    depth = lax.rem(z - x + NZ, NZ)
    is_source = lax.rem(depth, 4) == 0

    old = lax.broadcasted_iota(jnp.int32, (256, 256), 0)
    new = lax.broadcasted_iota(jnp.int32, (256, 256), 1)
    order = (old // 32 == (new // 16) % 8) & ((old // 16) % 2 == new // 128) & (old % 16 == new % 16)
    order = jnp.where(order, 1.0, 0.0)

    fetch[0].wait()

    @pl.when(is_source)
    def _():
        W[0, role, y_lo, core] = win[:16]
        W[1, role, y_lo, core] = win[16:]

    fetch[1].wait()
    for b in range(4):
        lanes = pl.ds(b * 256, 256)
        wout[:, lanes] = jnp.dot(wout[:, lanes], order.astype(BF16), preferred_element_type=F32).astype(BF16)
    WO[z, y_lo, core, :, :LB] = wout[:, :LB]

    @pl.when(is_source)
    def _():
        WO[z, y_lo, core, :, LB:] = wout[:, LB:]

    fetch[2].wait()
    pl.semaphore_wait(barrier, len(friends))

    back = pl.ds(LB, D - LB)
    front = pl.ds(0, LB)
    far_first = (4, 3, 5, 2, 6, 1, 7)

    def zin(c, k):
        piece = W.at[c, role, y_lo, core]
        return remote(piece, piece, zin_s.at[c, k], zin_r.at[c, role], at_z(k))

    def zo(k):
        piece = WO.at[z, y_lo, core, :, back]
        return remote(piece, piece, zo_s.at[k], zo_r.at[role], at_z(k))

    @pl.when(is_source)
    def _():
        for c in (0, 1):
            for k in far_first:
                zin(c, k).start()
        for k in far_first:
            zo(k).start()

    def yb(j):
        piece = WO.at[z, y_lo, core, :, front]
        return remote(piece, piece, yb_s.at[j], yb_r.at[j], at_y((0, 1, 7, 2)[j]))

    for j in (3, 1, 2):
        yb(j).start()

    tail = remote(fbuf.at[pl.ds(ROWS, HALO)], fbuf.at[pl.ds(0, HALO)], halo_s.at[0], halo_r.at[0], after)
    head = remote(fbuf.at[pl.ds(HALO, HALO)], fbuf.at[pl.ds(HALO + ROWS, HALO)], halo_s.at[1], halo_r.at[1], before)
    tail.start()
    head.start()

    for copy in fetch[3:]:
        copy.wait()
    for b in range(4):
        lanes = pl.ds(b * 256, 256)
        for first, src in ((0, raw_taps), (32, raw_scale), (40, raw_shift)):
            params[pl.ds(first, src.shape[0]), lanes] = jnp.dot(
                src[:, lanes], order, precision=lax.Precision.HIGHEST, preferred_element_type=F32
            )

    def normalize(row, count, keep):
        values = fbuf[pl.ds(row, count)].astype(F32)
        average = jnp.mean(values, axis=1, keepdims=True)
        centred = values - average
        variance = jnp.mean(centred * centred, axis=1, keepdims=True)
        result = centred * lax.rsqrt(variance + 1e-05) * gain[...]
        if keep is not None:
            result = jnp.where(keep, result, 0.0)
        normed[pl.ds(row, count)] = result.astype(BF16)

    for i in range(ROWS // 128):
        normalize(HALO + i * 128, 128, None)
    tail.wait_recv()
    head.wait_recv()
    normalize(0, HALO, tm > 0)
    normalize(HALO + ROWS, HALO, tm < 2 * NY * NZ - 1)

    near = jnp.where((depth <= 2) | (depth >= 6), 0, 1)
    roles = (near, 1 - near)

    def line(j):
        return lax.rem(y_lo + (0, 3, 1, 2)[j], NY)

    def yin(c, r, j):
        piece = W.at[c, r, y_lo, core]
        device = {1: at_y(1), 2: at_y(7), 3: at_y(2 + 4 * r)}[j]
        return remote(piece, piece, yin_s.at[c, r, j], yin_r.at[c, r, j], device)

    def yin_arrival(c, r, j):
        piece = W.at[c, r, line(j), core]
        return remote(piece, piece, yin_s.at[c, r, j], yin_r.at[c, r, j], partner)

    def din(c, r, j):
        piece = W.at[c, r, line(j), core]
        return remote(piece, piece, din_s.at[c, r, j], din_r.at[c, r, j], partner)

    def din_arrival(c, r, j):
        piece = W.at[c, r, line(j), 1 - core]
        return remote(piece, piece, din_s.at[c, r, j], din_r.at[c, r, j], partner)

    for c in (0, 1):
        for r in roles:

            @pl.when(depth != 4 * r)
            def _(c=c, r=r):
                piece = W.at[c, r, y_lo, core]
                remote(piece, piece, zin_s.at[c, 0], zin_r.at[c, r], partner).wait_recv()

            for j in (3, 1, 2):
                yin(c, r, j).start()
            din(c, r, 0).start()

    def xo(r, w):
        piece = WO.at[x + 4 * r, y_lo, core, :, back]
        return remote(piece, piece, xo_s.at[r, w], xo_r.at[r, w], at_x((2, 1, 3)[w]))

    for r in (0, 1):

        @pl.when(depth != 4 * r)
        def _(r=r):
            piece = WO.at[x + 4 * r, y_lo, core, :, back]
            remote(piece, piece, zo_s.at[0], zo_r.at[r], partner).wait_recv()

        for w in range(3):
            xo(r, w).start()

    for j in (1, 2, 3):
        piece = WO.at[z, line(j), core, :, front]
        remote(piece, piece, yb_s.at[j], yb_r.at[j], partner).wait_recv()

    def zb(k):
        piece = WO.at[z, :, core, :, front]
        return remote(piece, piece, zb_s.at[k], zb_r.at[k], at_z(k))

    for k in far_first:
        zb(k).start()

    def lift(c):
        columns = jnp.concatenate([W[c, 0].reshape(128, D), W[c, 1].reshape(128, D)], axis=0)
        lifted = lax.dot_general(normed[...], columns, NT, preferred_element_type=F32)
        G[x, c] = (lifted[:, :128] * sigmoid(lifted[:, 128:])).astype(BF16)

    parts = (pl.ds(0, SPAN // 2), pl.ds(SPAN // 2, SPAN // 2))

    def x_copy(c, way, p):
        piece = G.at[x, c, parts[p]]
        return remote(piece, piece, x_s.at[c, way, p], x_r.at[c, way, p], at_x((1, 3)[way]))

    def x_arrival(c, way, p):
        piece = G.at[lax.rem(x + (3, 1)[way], NX), c, parts[p]]
        return remote(piece, piece, x_s.at[c, way, p], x_r.at[c, way, p], partner)

    def x_forward(c, p):
        piece = G.at[lax.rem(x + (3, 1)[p], NX), c, parts[p]]
        return remote(piece, piece, xf_s.at[c, p], xf_r.at[c, p], at_x((1, 3)[p]))

    def x_far(c, p):
        piece = G.at[lax.rem(x + 2, NX), c, parts[p]]
        return remote(piece, piece, xf_s.at[c, p], xf_r.at[c, p], partner)

    def lift_and_send(c):
        for j in (1, 2, 3):
            for r in roles:
                yin_arrival(c, r, j).wait_recv()
                din(c, r, j).start()
        for j in range(4):
            for r in (0, 1):
                din_arrival(c, r, j).wait_recv()
        lift(c)
        for p in (0, 1):
            for way in (0, 1):
                x_copy(c, way, p ^ way).start()

    lift_and_send(0)

    for w in range(3):
        for r in (0, 1):
            piece = WO.at[lax.rem(x + (2, 3, 1)[w], NX) + 4 * r, y_lo, core, :, back]
            remote(piece, piece, xo_s.at[r, w], xo_r.at[r, w], partner).wait_recv()

    full = WO.at[:, y_lo, core, :, back]
    low, high = WO.at[pl.ds(0, NZ // 2), y_lo, core, :, back], WO.at[pl.ds(NZ // 2, NZ // 2), y_lo, core, :, back]
    yo = [
        remote(low, low, yo_s.at[2], yo_r.at[2], at_y(2)),
        remote(high, high, yo_s.at[3], yo_r.at[3], at_y(6)),
        remote(full, full, yo_s.at[0], yo_r.at[0], at_y(1)),
        remote(full, full, yo_s.at[1], yo_r.at[1], at_y(7)),
    ]
    for copy in yo:
        copy.start()

    def do(j):
        piece = WO.at[:, line(j), core, :, back]
        return remote(piece, piece, do_s.at[j], do_r.at[j], partner)

    do(0).start()

    lift_and_send(1)

    row0 = tm * ROWS
    span_low, span_high = start[0], start[0] + length[0]

    def occluded(begin, count):
        position = begin + lax.broadcasted_iota(jnp.int32, (count, 1), 0)
        return (position >= span_low) & (position < span_high)

    def convolve(step, c):
        owner = lax.rem(x + step, NX)
        lanes = pl.ds(pl.multiple_of(owner * 256 + c * 128, 128), 128)
        conv_in[...] = jnp.where(occluded(row0 - HALO, SPAN), 0.0, G[owner, c].astype(F32))

        @pl.loop(0, ROWS // CONV_ROWS)
        def _(i):
            row = pl.multiple_of(i * CONV_ROWS, CONV_ROWS)
            total = None
            for j in range(TAPS):
                term = conv_in[pl.ds(row + j + 1, CONV_ROWS)] * params[pl.ds(j, 1), lanes]
                total = term if total is None else total + term
            value = total * params[pl.ds(32, 1), lanes] + params[pl.ds(40, 1), lanes]
            act[owner, pl.ds(row, CONV_ROWS), pl.ds(c * 128, 128)] = (value * sigmoid(value)).astype(BF16)

    def product(step, n, first=0, count=256):
        owner = lax.rem(x + step, NX)
        depths = pl.ds(pl.multiple_of(owner * 256 + first, 128), count)
        columns = WO[2 * n : 2 * n + 2, :, :, :, depths].reshape(256, count)
        return lax.dot_general(act[owner, :, first : first + count], columns, NT, preferred_element_type=F32)

    convolve(0, 0)
    convolve(0, 1)
    for p in (0, 1):
        x_arrival(0, p, p).wait_recv()
        x_forward(0, p).start()
    for p in (0, 1):
        x_arrival(0, p, 1 - p).wait_recv()
    convolve(1, 0)
    convolve(3, 0)

    for p in (0, 1):
        x_arrival(1, p, p).wait_recv()
        x_forward(1, p).start()

    for k in range(1, NZ):
        piece = WO.at[lax.rem(z + NZ - k, NZ), :, core, :, front]
        remote(piece, piece, zb_s.at[k], zb_r.at[k], partner).wait_recv()
    mine = WO.at[:, :, core, :, front]
    db = remote(mine, mine, db_s.at[0], db_r.at[0], partner)
    db.start()

    for p in (0, 1):
        x_arrival(1, p, 1 - p).wait_recv()
    convolve(1, 1)
    convolve(3, 1)

    for j in (1, 2):
        piece = WO.at[:, line(j), core, :, back]
        remote(piece, piece, yo_s.at[0], yo_r.at[j - 1], partner).wait_recv()
        do(j).start()
    for h in (0, 1):
        piece = WO.at[pl.ds(h * 4, 4), line(3), core, :, back]
        remote(piece, piece, yo_s.at[0], yo_r.at[2 + h], partner).wait_recv()
    do(3).start()

    for p in (0, 1):
        x_far(0, p).wait_recv()
    convolve(2, 0)

    for j in range(4):
        piece = WO.at[:, line(j), 1 - core, :, back]
        remote(piece, piece, do_s.at[j], do_r.at[j], partner).wait_recv()
    theirs = WO.at[:, :, 1 - core, :, front]
    remote(theirs, theirs, db_s.at[0], db_r.at[0], partner).wait_recv()

    for n in range(4):
        acc[n] = product(0, n) + product(1, n) + product(3, n) + product(2, n, 0, 128)

    for p in (0, 1):
        x_far(1, p).wait_recv()
    convolve(2, 1)

    for n in range(4):
        lanes = pl.ds(n * 256, 256)
        masked = jnp.where(occluded(row0, ROWS), 0.0, fbuf[pl.ds(HALO, ROWS), lanes].astype(F32))
        out[:, lanes] = (masked + (acc[n] + product(2, n, 128, 128))).astype(BF16)

    @pl.when(is_source)
    def _():
        for k in far_first:
            zin(0, k).wait_send()
            zin(1, k).wait_send()
            zo(k).wait_send()

    tail.wait_send()
    head.wait_send()
    for c in (0, 1):
        for r in (0, 1):
            for j in (1, 2, 3):
                yin(c, r, j).wait_send()
            for j in range(4):
                din(c, r, j).wait_send()
        for p in (0, 1):
            for way in (0, 1):
                x_copy(c, way, p).wait_send()
            x_forward(c, p).wait_send()
    for r in (0, 1):
        for w in range(3):
            xo(r, w).wait_send()
    for j in (1, 2, 3):
        yb(j).wait_send()
    for k in far_first:
        zb(k).wait_send()
    for copy in yo:
        copy.wait_send()
    for j in range(4):
        do(j).wait_send()
    db.wait_send()


def module(frames, span_start, span_length, ln_gain, w_in, taps, bn_scale, bn_shift, w_out):
    hbm = pl.BlockSpec(memory_space=pl.ANY)
    dma = pltpu.SemaphoreType.DMA
    return pl.pallas_call(
        kernel,
        name="conformer_conv",
        out_shape=pltpu.VMEM((ROWS, D), BF16),
        in_specs=[hbm] * 9,
        out_specs=pl.BlockSpec(memory_space=pltpu.VMEM),
        scratch_shapes=[
            pltpu.VMEM((SPAN, D), BF16),
            pltpu.VMEM((SPAN, D), BF16),
            pltpu.VMEM((VAL, D), BF16),
            pltpu.VMEM((OUT, D), BF16),
            pltpu.VMEM((2, 2, NY, 2, OUT, D), BF16),
            pltpu.VMEM((NZ, NY, 2, OUT, D), BF16),
            pltpu.VMEM((NX, 2, SPAN, 128), BF16),
            pltpu.VMEM((SPAN, 128), F32),
            pltpu.VMEM((NX, ROWS, 256), BF16),
            pltpu.VMEM((4, ROWS, 256), F32),
            pltpu.VMEM((1, D), F32),
            pltpu.VMEM((TAPS, D), F32),
            pltpu.VMEM((1, D), F32),
            pltpu.VMEM((1, D), F32),
            pltpu.VMEM((48, D), F32),
            pltpu.SMEM((1,), jnp.int32),
            pltpu.SMEM((1,), jnp.int32),
            dma((9,)),
            dma((2,)), dma((2,)),
            dma((2, NZ)), dma((2, 2)),
            dma((2, 2, 4)), dma((2, 2, 4)),
            dma((2, 2, 4)), dma((2, 2, 4)),
            dma((2, 2, 2)), dma((2, 2, 2)),
            dma((2, 2)), dma((2, 2)),
            dma((NZ,)), dma((2,)),
            dma((2, 3)), dma((2, 3)),
            dma((4,)), dma((4,)),
            dma((4,)), dma((4,)),
            dma((4,)), dma((4,)),
            dma((NZ,)), dma((NZ,)),
            dma((1,)), dma((1,)),
        ],
        compiler_params=pltpu.CompilerParams(
            collective_id=0, has_side_effects=True, vmem_limit_bytes=VMEM_BYTES
        ),
    )(
        span_start, span_length, frames, w_in.T, w_out.T, ln_gain.reshape(1, D), taps,
        bn_scale.reshape(1, D), bn_shift.reshape(1, D),
    )


def solution(mesh):
    return jax.shard_map(
        module,
        mesh=mesh,
        in_specs=(P("tm", None), P("var"), P("var"), P(), P(None, "tm"), P(), P(), P(), P(None, "tm")),
        out_specs=P(("var", "tm"), None),
        check_vma=False,
    )
```
